32 devices in a mesh: ctx: 8 (over z, x), grp: 4 (over y, core).
Axes of the slice: x: 2, y: 2, z: 4, core: 2. Of those that a mesh axis runs over, the one named last changes fastest.
Arguments:
- query_heads: bfloat16 [4096, 2048], P('ctx', 'grp'), may hold values from -6 to 6
- key_heads: bfloat16 [4096, 2048], P('ctx', 'grp'), may hold values from -6 to 6
- value_heads: bfloat16 [4096, 2048], P('ctx', 'grp'), may hold values from -6 to 6
- log_decay: float32 [16, 4096], P('grp', 'ctx'), may hold values from -1 to 0
- residual: bfloat16 [4096, 2048], P(('ctx', 'grp')), may hold values from -4 to 4
- out_weight: bfloat16 [2048, 2048], replicated, may hold values from -0.5 to 0.5
- norm_gain: float32 [2048], replicated, may hold values from 0.25 to 1.75
- expert_ids: int32 [4096, 6], P(('ctx', 'grp')), may hold values from 0 to 63, all different within a row; in each aligned block of 128 rows (0 to 127, 128 to 255, ...) at most 15 rows name the same one
- gate_weights: float32 [4096, 6], P(('ctx', 'grp')), may hold values from 0.1 to 1
- gate_proj: bfloat16 [64, 2048, 1408], P('ctx', None, 'grp'), may hold values from -0.125 to 0.125
- up_proj: bfloat16 [64, 2048, 1408], P('ctx', None, 'grp'), may hold values from -0.125 to 0.125
- down_proj: bfloat16 [64, 1408, 2048], P('ctx', 'grp'), may hold values from -0.15625 to 0.15625
Outputs:
- attended: bfloat16 [4096, 2048], P(('ctx', 'grp'))
- layer_out: bfloat16 [4096, 2048], P(('ctx', 'grp'))
The draws below stay inside these ranges and needn't reach their ends.
Inputs may be any that keep to these rules, and one draw needn't show every extreme that they name: `expert_ids`: each token names 6 different experts. In each aligned block of 128 tokens no expert is named by more than 15 tokens, and that bound is reached.
All inputs are finite; a program needn't handle non-finite values.
Results may differ from the reference program's by a relative error of at most 0.02.
Values may be sent and summed in bfloat16 or wider, within the bound.
A program may use at most 128 MiB of HBM per device.

```python
import math
import jax
import jax.numpy as jnp
import numpy as np
from jax import lax

D = 2048
HEAD_COUNT = 16
HD = 128
E = 64
FF = 1408
TOPK = 6
TOK_DEV = 512
TOKENS = 4096
ROWS = 128
CAP = 15
N_GRP = 4


def draw_log_decay(key, part):
    random_subkeys = jax.random.split(jax.random.fold_in(key, 17), 7)
    ordering = jax.random.permutation(random_subkeys[0], HEAD_COUNT)
    slow_count = HEAD_COUNT // 2
    slow_head = ordering < slow_count
    slow_rate = jnp.exp(jax.random.uniform(random_subkeys[1], (HEAD_COUNT,), jnp.float32, math.log(0.05 / TOKENS), math.log(0.3 / TOKENS)))
    fast_rate = jnp.exp(jax.random.uniform(random_subkeys[2], (HEAD_COUNT,), jnp.float32, math.log(0.02), math.log(0.1)))
    decay_rate = jnp.where(slow_head, slow_rate, fast_rate)
    segments = TOKENS // TOK_DEV
    segment_factor = jnp.exp(jax.random.uniform(random_subkeys[3], (HEAD_COUNT, segments), jnp.float32, math.log(0.5), math.log(2.0)))
    jitter = jax.random.uniform(random_subkeys[4], (HEAD_COUNT, TOKENS), jnp.float32, 0.5, 1.5)
    decay_floor = -decay_rate[:, None] * jnp.repeat(segment_factor, TOK_DEV, axis=1) * jitter
    widening_factor = TOKENS // 3
    spike_position = jnp.arange(3, dtype=jnp.int32) * widening_factor + jax.random.randint(random_subkeys[5], (3,), 0, widening_factor)
    spike_retain = jax.random.uniform(random_subkeys[6], (HEAD_COUNT, 3), jnp.float32, 0.5, 0.8)
    token_positions = jnp.arange(TOKENS, dtype=jnp.int32)
    spike_matches = (token_positions[None, :] == spike_position[:, None]).astype(jnp.float32)
    decay_floor = decay_floor + jnp.dot(jnp.log(spike_retain), spike_matches)
    return decay_floor.astype(jnp.float32)


def block_scale(rng, extent, shards, low, largest):
    loudness, own = 1.0, jax.random.fold_in(rng, 6)
    for axis_at, parts in shards:
        draws = jnp.exp(jax.random.uniform(jax.random.fold_in(own, axis_at), (parts,), jnp.float32, low / len(shards), largest / len(shards)))
        loudness = loudness * jnp.repeat(draws, extent[axis_at] // parts).reshape([-1 if axis == axis_at else 1 for axis in range(len(extent))])
    return loudness


def assign_block(rng, own, number, rows, amount, top, limit, lean):
    order = jax.random.permutation(rng, amount)
    heavy_load, ordinary = portions_of(amount, rows * top, limit, lean, True), portions_of(amount, rows * top, limit, lean, False)
    places = jnp.arange(amount)

    def named(lengths, offset_by):
        used = int((lengths > 0).sum())
        fixed = max(1, used // 4)
        shifted = fixed + (places - fixed + offset_by * (used - fixed)) % max(1, amount - fixed)
        return jnp.zeros((amount,), jnp.int32).at[order[jnp.where(places < fixed, places, shifted)]].set(jnp.asarray(lengths, jnp.int32))

    lengths = jnp.where(number % 4 == 0, named(heavy_load, number // 4), named(ordinary, number - number // 4 - 1))
    mixed = jax.random.permutation(jax.random.fold_in(own, 3), amount)
    giver, sink = mixed[0:amount // 2 * 2:2], mixed[1:amount // 2 * 2:2]
    room = jnp.minimum(lengths[giver] - 1, limit - lengths[sink]) // 2
    room = jnp.where((giver == order[0]) | (sink == order[0]) | (lengths[sink] == 0), 0, jnp.maximum(room, 0))
    shifted = jax.random.randint(jax.random.fold_in(own, 4), (amount // 2,), 0, 1 << 20) % (room + 1)
    lengths = lengths.at[giver].add(-shifted).at[sink].add(shifted)
    members = jnp.searchsorted(jnp.cumsum(lengths), jnp.arange(rows * top), side="right").astype(jnp.int32)
    table = members.reshape(top, rows).T
    table = table[jax.random.permutation(jax.random.fold_in(own, 1), rows)]
    offset_by = jax.random.randint(jax.random.fold_in(own, 2), (rows, 1), 0, top)
    return jnp.take_along_axis(table, (jnp.arange(top)[None, :] + offset_by) % top, axis=1)


def portions_of(number_of, total, most, skew, full):
    portions = [(1 << 20) // math.isqrt(grade ** skew) + 1 for grade in range(1, number_of + 1)]
    largest = most if full else min(most, max(-(-total // number_of), total * portions[0] // sum(portions)))
    least = 1 if total - largest >= number_of - 1 else 0
    holding, rest = [largest] + [least] * (number_of - 1), total - largest - least * (number_of - 1)
    while rest > 0:
        candidates = [i for i in range(1, number_of) if holding[i] < largest] or [i for i in range(1, number_of) if holding[i] < most]
        mass, budget = sum([portions[i] for i in candidates]), rest
        for i in candidates:
            more = min(most - holding[i], max(1, budget * portions[i] // mass), rest)
            holding[i] = holding[i] + more
            rest = rest - more
    return np.array(holding)


def normal_values(rng, extent, scale, bound, cuts=(), held_as=jnp.bfloat16):
    drawn = scale * jax.random.normal(rng, extent, jnp.float32)
    if cuts:
        drawn = drawn * block_scale(rng, extent, cuts, -0.22, 0.18)
    return jnp.clip(drawn, -bound, bound).astype(held_as)


def setup_inputs(seed: int = 0) -> dict:
    streams_of = jax.random.split(jax.random.key(seed), 13)
    query_heads = normal_values(streams_of[0], (TOKENS, HEAD_COUNT * HD), 1.0, 6.0, ((0, 8), (1, 4)))
    key_heads = normal_values(streams_of[1], (TOKENS, HEAD_COUNT * HD), 1.0, 6.0, ((0, 8), (1, 4)))
    value_heads = normal_values(streams_of[2], (TOKENS, HEAD_COUNT * HD), 1.0, 6.0, ((0, 8), (1, 4)))
    log_decay = draw_log_decay(jax.random.fold_in(streams_of[12], 71), 0)
    residual = normal_values(streams_of[4], (TOKENS, D), 0.5, 4.0, ((0, 32),))
    out_weight = normal_values(streams_of[5], (HEAD_COUNT * HD, D), HD ** -0.5, 0.5)
    norm_gain = jnp.clip(1.0 + 0.15 * jax.random.normal(streams_of[6], (D,), jnp.float32), 0.25, 1.75)
    expert_ids_keys = jax.random.split(jax.random.fold_in(streams_of[7], 1), TOKENS // ROWS)
    expert_ids_turns = jax.random.permutation(jax.random.fold_in(streams_of[7], 3), TOKENS // ROWS)
    expert_ids = jax.vmap(lambda own, number: assign_block(jax.random.fold_in(streams_of[7], 2), own, number, ROWS, E, TOPK, CAP, 2))(expert_ids_keys, expert_ids_turns).reshape((TOKENS, TOPK))
    gate_weights = jnp.clip(0.1 + 0.9 * jax.random.uniform(streams_of[8], (TOKENS, TOPK), jnp.float32) ** block_scale(streams_of[8], (TOKENS, TOPK), ((0, 32),), -0.2, 0.2), 0.1, 1.0)
    gate_proj = normal_values(streams_of[9], (E, D, FF), D ** -0.5, 0.125, ((0, 8), (2, 4)))
    up_proj = normal_values(streams_of[10], (E, D, FF), D ** -0.5, 0.125, ((0, 8), (2, 4)))
    down_proj = normal_values(streams_of[11], (E, FF, D), FF ** -0.5, 0.15625, ((0, 8), (1, 4)))
    return {"query_heads": query_heads, "key_heads": key_heads, "value_heads": value_heads, "log_decay": log_decay, "residual": residual, "out_weight": out_weight, "norm_gain": norm_gain, "expert_ids": expert_ids, "gate_weights": gate_weights, "gate_proj": gate_proj, "up_proj": up_proj, "down_proj": down_proj}


def feature_map(values):
    return (jax.nn.elu(values.astype(jnp.float32)) + 1.0).astype(jnp.bfloat16)

def block_attention(feat_query, feat_key, value_rows, decay_rows, preceding_state, prior_norm):
    length = feat_query.shape[0]
    cumulative = jnp.cumsum(decay_rows, axis=1)
    block_total = cumulative[:, -1]
    query_wide = feat_query.astype(jnp.float32)
    key_wide = feat_key.astype(jnp.float32)
    value_broad = value_rows.astype(jnp.float32)
    scores = jnp.einsum('thd,shd->hts', query_wide, key_wide)
    row_index = lax.broadcasted_iota(jnp.int32, (length, length), 0)
    col_index = lax.broadcasted_iota(jnp.int32, (length, length), 1)
    causal = (col_index <= row_index)[None]
    spread = cumulative[:, :, None] - cumulative[:, None, :]
    weights = jnp.where(causal, scores * jnp.exp(jnp.where(causal, spread, 0.0)), 0.0)
    inner_den = lax.optimization_barrier(jnp.sum(weights, axis=2)).T
    inner_num = jnp.einsum('hts,shd->thd', weights.astype(jnp.bfloat16).astype(jnp.float32), value_broad)
    query_damping = query_wide * jnp.exp(cumulative).T[:, :, None]
    outer_numerator = jnp.einsum('cnm,nmp->cnp', query_damping, preceding_state, precision=lax.Precision.HIGHEST)
    outer_den = jnp.einsum('thk,hk->th', query_damping, prior_norm, precision=lax.Precision.HIGHEST)
    mixed_rows = ((inner_num + outer_numerator) / (inner_den + outer_den)[:, :, None]).astype(jnp.bfloat16)
    trailing_keys = key_wide * jnp.exp(block_total[:, None] - cumulative).T[:, :, None]
    shard_state = jnp.einsum('jfi,jfx->fix', trailing_keys.astype(jnp.bfloat16).astype(jnp.float32), value_broad)
    local_norm = lax.optimization_barrier(jnp.sum(trailing_keys, axis=0))
    return (mixed_rows.reshape(length, -1), block_total, shard_state, local_norm)

def route_block(block_ids, block_gates, block_normed):
    onehot = (block_ids[:, :, None] == jnp.arange(E, dtype=jnp.int32)).astype(jnp.int32)
    flat_hits = onehot.reshape(ROWS * TOPK, E)
    earlier = jnp.cumsum(flat_hits, axis=0) - flat_hits
    slot_index = lax.optimization_barrier(jnp.sum(earlier * flat_hits, axis=1)).reshape(ROWS, TOPK)
    target = block_ids * CAP + slot_index
    placed = (target[:, :, None] == jnp.arange(E * CAP, dtype=jnp.int32)).astype(jnp.float32)
    dispatch_rows = lax.optimization_barrier(jnp.sum(placed, axis=1)).astype(jnp.bfloat16)
    combiner = lax.optimization_barrier(jnp.sum(placed * block_gates.astype(jnp.bfloat16).astype(jnp.float32)[:, :, None], axis=1)).astype(jnp.bfloat16)
    buffer = jnp.dot(dispatch_rows.T, block_normed, preferred_element_type=jnp.float32).astype(jnp.bfloat16)
    return (buffer.reshape(E, CAP, D), combiner)

def reference(query_heads, key_heads, value_heads, log_decay, residual, out_weight, norm_gain, expert_ids, gate_weights, gate_proj, up_proj, down_proj):
    blocks = TOKENS // TOK_DEV
    feat_query = feature_map(query_heads).reshape(blocks, TOK_DEV, HEAD_COUNT, HD)
    feat_key = feature_map(key_heads).reshape(blocks, TOK_DEV, HEAD_COUNT, HD)
    value_rows = value_heads.reshape(blocks, TOK_DEV, HEAD_COUNT, HD)
    decay_rows = log_decay.reshape(HEAD_COUNT, blocks, TOK_DEV).transpose(1, 0, 2)

    def advance(running, packed):
        preceding_state, prior_norm = running
        mixed_rows, block_total, shard_state, local_norm = block_attention(packed[0], packed[1], packed[2], packed[3], preceding_state, prior_norm)
        factor = jnp.exp(block_total)
        return ((factor[:, None, None] * preceding_state + shard_state, factor[:, None] * prior_norm + local_norm), mixed_rows)
    start_state = (jnp.zeros((HEAD_COUNT, HD, HD), jnp.float32), jnp.zeros((HEAD_COUNT, HD), jnp.float32))
    _, head_rows = lax.scan(advance, start_state, (feat_query, feat_key, value_rows, decay_rows))
    head_rows = head_rows.reshape(TOKENS, HEAD_COUNT * HD)
    projected = jnp.dot(head_rows, out_weight, preferred_element_type=jnp.float32)
    attended = (residual.astype(jnp.float32) + projected).astype(jnp.bfloat16)
    widened = attended.astype(jnp.float32)
    normed = (widened * lax.rsqrt(lax.optimization_barrier(jnp.mean(widened * widened, axis=1, keepdims=True)) + 1e-06) * norm_gain).astype(jnp.bfloat16)
    groups = TOKENS // ROWS
    buffers, combiners = lax.map(lambda packed: route_block(packed[0], packed[1], packed[2]), (expert_ids.reshape(groups, ROWS, TOPK), gate_weights.reshape(groups, ROWS, TOPK), normed.reshape(groups, ROWS, D)))
    quarter_width = FF // N_GRP

    def run_expert(packed):
        rows_in, gate_block, up_block, down_block = packed
        flat_rows = rows_in.reshape(groups * CAP, D)
        summed = jnp.zeros((groups * CAP, D), jnp.float32)
        for quarter in range(N_GRP):
            lower_col = quarter * quarter_width
            upper_col = lower_col + quarter_width
            gate_part = jnp.dot(flat_rows, gate_block[:, lower_col:upper_col], preferred_element_type=jnp.float32)
            up_part = jnp.dot(flat_rows, up_block[:, lower_col:upper_col], preferred_element_type=jnp.float32)
            hidden = (jax.nn.silu(gate_part) * up_part).astype(jnp.bfloat16)
            part_out = jnp.dot(hidden, down_block[lower_col:upper_col], preferred_element_type=jnp.float32).astype(jnp.bfloat16)
            summed = summed + part_out.astype(jnp.float32)
        return summed.astype(jnp.bfloat16).reshape(groups, CAP, D)
    expert_out = lax.map(run_expert, (jnp.swapaxes(buffers, 0, 1), gate_proj, up_proj, down_proj))
    returned = jnp.swapaxes(expert_out, 0, 1).reshape(groups, E * CAP, D)
    expert_mix = lax.map(lambda packed: jnp.dot(packed[0], packed[1], preferred_element_type=jnp.float32), (combiners, returned))
    layer_out = (widened + expert_mix.reshape(TOKENS, D)).astype(jnp.bfloat16)
    return (attended, layer_out)
```

```python
import functools

import jax
import jax.numpy as jnp
from jax import lax
from jax.experimental import pallas as pl
from jax.experimental.pallas import tpu as pltpu
from jax.sharding import PartitionSpec as P

D = 2048
HD = 128
E = 64
TOPK = 6


MESH = pl.DeviceIdType.MESH
VMEM_TOKENS = 4096


class Grid:
    def __init__(self, nz):
        ctx, grp = lax.axis_index("ctx"), lax.axis_index("grp")
        self.nz = nz
        self.z, self.x = ctx // 2, ctx % 2
        self.y, self.c = grp // 2, grp % 2
        self.fx, self.fy, self.fc = 1 - self.x, 1 - self.y, 1 - self.c

    def turn(self, dz):
        return lax.rem(self.z + dz, self.nz)

    def meet(self):
        barrier = pltpu.get_barrier_semaphore()
        partners = [device(self.turn(dz), self.x, self.y, self.c) for dz in range(1, self.nz)]
        partners += [
            device(self.z, self.fx, self.y, self.c),
            device(self.z, self.x, self.fy, self.c),
            device(self.z, self.x, self.y, self.fc),
        ]
        for partner in partners:
            pl.semaphore_signal(barrier, inc=1, device_id=partner, device_id_type=MESH)
        pl.semaphore_wait(barrier, len(partners))


def device(z, x, y, c):
    return (z * 2 + x, y * 2 + c)


def block_at(z, x, y, c):
    return (z * 2 + x) * 4 + y * 2 + c


def gather_kernel(nz, own_ref, out_ref, send_sem, recv_sem, core_sem, local_sem):
    at = Grid(nz)
    half = own_ref.shape[0] // 2
    at.meet()
    sends = []

    def send(src, dst, sem, to):
        copy = pltpu.make_async_remote_copy(
            src_ref=src,
            dst_ref=dst,
            send_sem=send_sem.at[len(sends)],
            recv_sem=sem,
            device_id=to,
            device_id_type=MESH,
        )
        copy.start()
        sends.append(copy)

    def rows_of(z, x, y, c, h):
        block = out_ref.at[block_at(z, x, y, c)]
        return block if h is None else block.at[pl.ds(h * half, half)]

    def sem_of(sems, z, x, y, h):
        return sems.at[((z * 2 + x) * 2 + y) * 2 + (0 if h is None else h)]

    def forward(z, x, y, h, to, src=None):
        ref = rows_of(z, x, y, at.c, h)
        send(ref if src is None else src, ref, sem_of(recv_sem, z, x, y, h), to)

    def forward_core(z, x, y, h, src=None):
        ref = rows_of(z, x, y, at.c, h)
        send(
            ref if src is None else src,
            ref,
            sem_of(core_sem, z, x, y, h),
            device(at.z, at.x, at.y, at.fc),
        )

    def arrive(sems, z, x, y, c, h):
        ref = rows_of(z, x, y, c, h)
        pltpu.make_async_copy(ref, ref, sem_of(sems, z, x, y, h)).wait()

    local = pltpu.make_async_copy(own_ref, out_ref.at[block_at(at.z, at.x, at.y, at.c)], local_sem)
    local.start()
    for dz in range(1, nz):
        forward(at.z, at.x, at.y, None, device(at.turn(dz), at.x, at.y, at.c), own_ref)

    to_x = device(at.z, at.fx, at.y, at.c)
    to_y = device(at.z, at.x, at.fy, at.c)

    def column(dz):
        z = at.turn(dz)
        if dz:
            arrive(recv_sem, z, at.x, at.y, at.c, None)
        src = None if dz else own_ref
        forward(z, at.x, at.y, None, to_x, src)
        forward(z, at.x, at.y, None, to_y, src)
        forward_core(z, at.x, at.y, None, src)

    def turned(dz):
        z = at.turn(dz)
        arrive(recv_sem, z, at.fx, at.y, at.c, None)
        forward(z, at.fx, at.y, 0, to_y)
        forward_core(z, at.fx, at.y, None)
        arrive(recv_sem, z, at.x, at.fy, at.c, None)
        forward(z, at.x, at.fy, 1, to_x)
        forward_core(z, at.x, at.fy, None)

    order = [0] + [d for k in range(1, nz) for d in sorted({k, nz - k}) if k <= nz - k]
    column(order[0])
    for before, now in zip(order, order[1:]):
        column(now)
        turned(before)
    turned(order[-1])
    for dz in order:
        z = at.turn(dz)
        for h in range(2):
            arrive(recv_sem, z, at.fx, at.fy, at.c, h)
            forward_core(z, at.fx, at.fy, h)
    for dz in order:
        z = at.turn(dz)
        arrive(core_sem, z, at.x, at.y, at.fc, None)
        arrive(core_sem, z, at.fx, at.y, at.fc, None)
        arrive(core_sem, z, at.x, at.fy, at.fc, None)
        arrive(core_sem, z, at.fx, at.fy, at.fc, 0)
        arrive(core_sem, z, at.fx, at.fy, at.fc, 1)
    for copy in sends:
        copy.wait_send()
    local.wait()


def gather_rows(own, nz):
    rows, width = own.shape
    blocks = nz * 8
    return pl.pallas_call(
        functools.partial(gather_kernel, nz),
        out_shape=jax.ShapeDtypeStruct((blocks, rows, width), own.dtype),
        in_specs=[pl.BlockSpec(memory_space=pltpu.VMEM)],
        out_specs=pl.BlockSpec(memory_space=pl.ANY),
        scratch_shapes=[
            pltpu.SemaphoreType.DMA((nz * 16,)),
            pltpu.SemaphoreType.DMA((nz * 8,)),
            pltpu.SemaphoreType.DMA((nz * 8,)),
            pltpu.SemaphoreType.DMA,
        ],
        compiler_params=pltpu.CompilerParams(collective_id=0, has_side_effects=True),
        name="gather_rows",
    )(own)


def combine_kernel(
    nz,
    combiner_ref,
    outs_ref,
    mix_ref,
    acc,
    core_in,
    diag_in,
    x_in,
    y_in,
    z_in,
    stage,
    stage_sem,
    send_sem,
    recv_sem,
    core_sem,
):
    at = Grid(nz)
    rows = acc.shape[1]
    half = rows // 2
    spots = [(z, x, y) for x, y in ((1, 1), (1, 0), (0, 1), (0, 0)) for z in range(1, nz + 1)]
    sends = []

    def where(spot):
        dz, dx, dy = spot
        return (
            at.turn(dz % nz),
            at.fx if dx else at.x,
            at.fy if dy else at.y,
        )

    def place(z, x, y):
        return (z * 2 + x) * 2 + y

    turns = [(spot, c) for spot in spots for c in (at.fc, at.c)]

    def load(i):
        spot, c = turns[i]
        return pltpu.make_async_copy(
            outs_ref.at[block_at(*where(spot), c)], stage.at[i % 3], stage_sem.at[i % 3]
        )

    load(0).start()
    load(1).start()
    at.meet()

    def send(src, dst, sem, to):
        copy = pltpu.make_async_remote_copy(
            src_ref=src,
            dst_ref=dst,
            send_sem=send_sem.at[len(sends)],
            recv_sem=sem,
            device_id=to,
            device_id_type=MESH,
        )
        copy.start()
        sends.append(copy)

    def arrive(ref, sem):
        pltpu.make_async_copy(ref, ref, sem).wait()

    def make(i):
        if i + 2 < len(turns):
            load(i + 2).start()
        load(i).wait()
        spot, c = turns[i]
        block = block_at(*where(spot), c)
        slot = i % 3

        @pl.loop(0, acc.shape[2] // 512)
        def _(k):
            cols = pl.ds(pl.multiple_of(k * 512, 512), 512)
            acc[block, :, cols] = jnp.dot(
                combiner_ref[block], stage[slot, :, cols], preferred_element_type=jnp.float32
            ).astype(acc.dtype)

        return block

    def add(block, h, others):
        first, count = (0, rows) if h is None else (h * half, half)

        @pl.loop(0, count // 16)
        def _(k):
            at_acc = pl.ds(pl.multiple_of(first + k * 16, 16), 16)
            total = acc[block, at_acc, :].astype(jnp.float32)
            for ref, lead in others:
                total = total + ref[lead, at_acc, :].astype(jnp.float32)
            acc[block, at_acc, :] = total.astype(acc.dtype)

    to_x = device(at.z, at.fx, at.y, at.c)
    to_y = device(at.z, at.x, at.fy, at.c)
    to_core = device(at.z, at.x, at.y, at.fc)
    for i in range(0, len(turns), 2):
        spot = turns[i][0]
        dz, dx, dy = spot
        z, x, y = where(spot)
        theirs = make(i)
        spare = place(z, x, y)
        send(acc.at[theirs], core_in.at[spare], core_sem.at[spare], to_core)
        mine = make(i + 1)
        arrive(core_in.at[spare], core_sem.at[spare])
        if dx and dy:
            add(mine, None, [(core_in, spare)])
            send(
                acc.at[mine, pl.ds(0, half)],
                diag_in.at[z, pl.ds(0, half)],
                recv_sem.at[z],
                to_y,
            )
            send(
                acc.at[mine, pl.ds(half, half)],
                diag_in.at[z, pl.ds(half, half)],
                recv_sem.at[nz + z],
                to_x,
            )
        elif dx:
            arrive(diag_in.at[z, pl.ds(0, half)], recv_sem.at[z])
            add(mine, 0, [(core_in, spare), (diag_in, z)])
            add(mine, 1, [(core_in, spare)])
            send(acc.at[mine], x_in.at[z], recv_sem.at[2 * nz + z], to_x)
        elif dy:
            arrive(diag_in.at[z, pl.ds(half, half)], recv_sem.at[nz + z])
            add(mine, 0, [(core_in, spare)])
            add(mine, 1, [(core_in, spare), (diag_in, z)])
            send(acc.at[mine], y_in.at[z], recv_sem.at[3 * nz + z], to_y)
        else:
            arrive(x_in.at[z], recv_sem.at[2 * nz + z])
            arrive(y_in.at[z], recv_sem.at[3 * nz + z])
            add(mine, None, [(core_in, spare), (x_in, z), (y_in, z)])
            if dz % nz:
                send(
                    acc.at[mine],
                    z_in.at[at.z],
                    recv_sem.at[4 * nz + at.z],
                    device(z, at.x, at.y, at.c),
                )
    others = [at.turn(dz) for dz in range(1, nz)]
    for z in others:
        arrive(z_in.at[z], recv_sem.at[4 * nz + z])
    own = block_at(at.z, at.x, at.y, at.c)

    @pl.loop(0, rows // 16)
    def _(k):
        part = pl.ds(pl.multiple_of(k * 16, 16), 16)
        total = acc[own, part, :].astype(jnp.float32)
        for z in others:
            total = total + z_in[z, part, :].astype(jnp.float32)
        mix_ref[part, :] = total

    for copy in sends:
        copy.wait_send()


def combine_rows(combiner, outs, nz):
    blocks, rows, slots = combiner.shape
    width = outs.shape[2]
    kind = outs.dtype
    return pl.pallas_call(
        functools.partial(combine_kernel, nz),
        out_shape=jax.ShapeDtypeStruct((rows, width), jnp.float32),
        in_specs=[pl.BlockSpec(memory_space=pltpu.VMEM), pl.BlockSpec(memory_space=pl.ANY)],
        out_specs=pl.BlockSpec(memory_space=pltpu.VMEM),
        scratch_shapes=[
            pltpu.VMEM((blocks, rows, width), kind),
            pltpu.VMEM((blocks // 2, rows, width), kind),
            pltpu.VMEM((nz, rows, width), kind),
            pltpu.VMEM((nz, rows, width), kind),
            pltpu.VMEM((nz, rows, width), kind),
            pltpu.VMEM((nz, rows, width), kind),
            pltpu.VMEM((3, slots, width), kind),
            pltpu.SemaphoreType.DMA((3,)),
            pltpu.SemaphoreType.DMA((nz * 10,)),
            pltpu.SemaphoreType.DMA((nz * 5,)),
            pltpu.SemaphoreType.DMA((nz * 4,)),
        ],
        compiler_params=pltpu.CompilerParams(
            collective_id=1, has_side_effects=True, vmem_limit_bytes=56 * 1024 * 1024
        ),
        name="combine_rows",
    )(combiner, outs)


def entering(array, axis, combine, identity):
    count, index = (lax.axis_size(axis), lax.axis_index(axis))
    everything = jax.tree.map(
        lambda part, kind: lax.all_gather(part.astype(kind), axis),
        array,
        (jnp.bfloat16, jnp.bfloat16, jnp.bfloat16),
    )
    start = jax.tree.map(
        lambda part, zero: jnp.broadcast_to(jnp.asarray(zero, part.dtype), part.shape),
        array,
        identity,
    )

    def lap(k, before):
        reached = k < index
        new = combine(
            before, jax.tree.map(lambda part, own: part[k].astype(own.dtype), everything, array)
        )
        return jax.tree.map(lambda a, b: jnp.where(reached, a, b), new, before)

    return lax.fori_loop(0, count, lap, start)


def feature_map(values):
    return (jax.nn.elu(values.astype(jnp.float32)) + 1.0).astype(jnp.bfloat16)


def summarize(feat_key, value_rows, log_decay):
    cumulative = jnp.cumsum(log_decay, axis=1)
    block_total = cumulative[:, -1]
    trailing_keys = (
        feat_key.astype(jnp.float32) * jnp.exp(block_total[:, None] - cumulative).T[:, :, None]
    )
    shard_state = jnp.einsum(
        "jfi,jfx->fix",
        trailing_keys.astype(jnp.bfloat16),
        value_rows,
        preferred_element_type=jnp.float32,
    )
    local_norm = jnp.sum(trailing_keys, axis=0)
    return (cumulative, block_total, shard_state, local_norm)


def block_output(feat_query, feat_key, value_rows, cumulative, preceding_state, prior_norm):
    length = feat_query.shape[0]
    scores = jnp.einsum("thd,shd->hts", feat_query, feat_key, preferred_element_type=jnp.float32)
    row_index = lax.broadcasted_iota(jnp.int32, (length, length), 0)
    col_index = lax.broadcasted_iota(jnp.int32, (length, length), 1)
    causal = (col_index <= row_index)[None]
    spread = cumulative[:, :, None] - cumulative[:, None, :]
    weights = jnp.where(causal, scores * jnp.exp(jnp.where(causal, spread, 0.0)), 0.0)
    inner_den = jnp.sum(weights, axis=2).T
    inner_num = jnp.einsum(
        "hts,shd->thd", weights.astype(jnp.bfloat16), value_rows, preferred_element_type=jnp.float32
    )
    query_damping = feat_query.astype(jnp.float32) * jnp.exp(cumulative).T[:, :, None]
    outer_numerator = jnp.einsum(
        "cnm,nmp->cnp", query_damping, preceding_state, precision=lax.Precision.HIGHEST
    )
    outer_den = jnp.einsum("thk,hk->th", query_damping, prior_norm, precision=lax.Precision.HIGHEST)
    mixed_rows = ((inner_num + outer_numerator) / (inner_den + outer_den)[:, :, None]).astype(
        jnp.bfloat16
    )
    return mixed_rows.reshape(length, -1)


def merge_states(earlier_part, later_part):
    first_total, first_state, first_norm = earlier_part
    second_total, second_state, second_norm = later_part
    factor = jnp.exp(second_total)
    return (
        first_total + second_total,
        factor[:, None, None] * first_state + second_state,
        factor[:, None] * first_norm + second_norm,
    )


def local_routes(expert_ids, gate_weights, row_count, local_experts, capacity):
    blocks = expert_ids.shape[0] // row_count
    own = lax.axis_index("ctx") * local_experts + jnp.arange(local_experts, dtype=jnp.int32)
    named = (expert_ids[:, :, None] == own).astype(jnp.float32)
    gates = jnp.sum(named * gate_weights.astype(jnp.float32)[:, :, None], axis=1)
    hits = jnp.sum(named, axis=1).reshape(blocks, row_count, local_experts)
    row = lax.broadcasted_iota(jnp.int32, (row_count, row_count), 0)
    col = lax.broadcasted_iota(jnp.int32, (row_count, row_count), 1)
    before = (col < row).astype(jnp.bfloat16)
    slot = jnp.einsum(
        "rs,bse->bre", before, hits.astype(jnp.bfloat16), preferred_element_type=jnp.float32
    )
    placed = jnp.where(
        (slot[:, :, :, None] == jnp.arange(capacity, dtype=jnp.float32)) & (hits[:, :, :, None] > 0),
        1.0,
        0.0,
    )
    combiner = placed * gates.reshape(blocks, row_count, local_experts, 1)
    flat = (blocks, row_count, local_experts * capacity)
    return placed.astype(jnp.bfloat16).reshape(flat), combiner.astype(jnp.bfloat16).reshape(flat)


def on_device(
    query_heads,
    key_heads,
    value_heads,
    log_decay,
    residual,
    out_weight,
    norm_gain,
    expert_ids,
    gate_weights,
    gate_proj,
    up_proj,
    down_proj,
):
    length = query_heads.shape[0]
    local_heads = query_heads.shape[1] // HD
    feat_query = feature_map(query_heads).reshape(length, local_heads, HD)
    feat_key = feature_map(key_heads).reshape(length, local_heads, HD)
    value_rows = value_heads.reshape(length, local_heads, HD)
    cumulative, block_total, shard_state, local_norm = summarize(feat_key, value_rows, log_decay)
    start_state = (
        jnp.zeros_like(block_total),
        jnp.zeros_like(shard_state),
        jnp.zeros_like(local_norm),
    )
    _, preceding_state, prior_norm = entering(
        (block_total, shard_state, local_norm), "ctx", merge_states, start_state
    )
    mixed_rows = block_output(
        feat_query, feat_key, value_rows, cumulative, preceding_state, prior_norm
    )
    head_rows = lax.all_to_all(mixed_rows, "grp", split_axis=0, concat_axis=1, tiled=True)
    projected = jnp.dot(head_rows, out_weight, preferred_element_type=jnp.float32)
    attended = (residual.astype(jnp.float32) + projected).astype(jnp.bfloat16)
    widened = attended.astype(jnp.float32)
    normed = (
        widened * lax.rsqrt(jnp.mean(widened * widened, axis=1, keepdims=True) + 1e-06) * norm_gain
    ).astype(jnp.bfloat16)
    row_count = expert_ids.shape[0]
    capacity = (5 * row_count * TOPK + 4 * E - 1) // (4 * E)
    capacity = (capacity + 15) // 16 * 16
    local_experts = gate_proj.shape[0]
    everyone = ("ctx", "grp")
    all_ids = lax.all_gather(expert_ids, everyone, axis=0, tiled=True)
    all_gates = lax.all_gather(gate_weights.astype(jnp.bfloat16), everyone, axis=0, tiled=True)
    placed, combiner = local_routes(all_ids, all_gates, row_count, local_experts, capacity)
    blocks = lax.axis_size("ctx") * lax.axis_size("grp")
    nz = lax.axis_size("ctx") // 2
    kernels = lax.axis_size("grp") == 4 and blocks * row_count <= VMEM_TOKENS
    if kernels:
        all_rows = gather_rows(normed, nz)
    else:
        all_rows = lax.all_gather(normed, everyone, axis=0, tiled=True)
    block_rows = jnp.einsum(
        "brs,brd->bsd",
        placed,
        all_rows.reshape(blocks, row_count, D),
        preferred_element_type=jnp.float32,
    ).astype(jnp.bfloat16).reshape(blocks, local_experts, capacity, D)
    gate_part = jnp.einsum(
        "secd,edf->secf", block_rows, gate_proj, preferred_element_type=jnp.float32
    )
    up_part = jnp.einsum("secd,edf->secf", block_rows, up_proj, preferred_element_type=jnp.float32)
    hidden = (jax.nn.silu(gate_part) * up_part).astype(jnp.bfloat16)
    partial_out = jnp.einsum(
        "secf,efd->secd", hidden, down_proj, preferred_element_type=jnp.float32
    ).astype(jnp.bfloat16)
    partial_rows = partial_out.reshape(blocks, local_experts * capacity, D)
    if kernels:
        expert_mix = combine_rows(combiner, partial_rows, nz)
    else:
        partial_mix = jnp.einsum(
            "brs,bsd->brd", combiner, partial_rows, preferred_element_type=jnp.float32
        ).astype(jnp.bfloat16)
        expert_mix = lax.psum_scatter(
            partial_mix.reshape(-1, D), everyone, scatter_dimension=0, tiled=True
        ).astype(jnp.float32)
    layer_out = (widened + expert_mix).astype(jnp.bfloat16)
    return (attended, layer_out)


def solution(mesh):
    placed = (
        P("ctx", "grp"),
        P("ctx", "grp"),
        P("ctx", "grp"),
        P("grp", "ctx"),
        P(("ctx", "grp"), None),
        P(),
        P(),
        P(("ctx", "grp"), None),
        P(("ctx", "grp"), None),
        P("ctx", None, "grp"),
        P("ctx", None, "grp"),
        P("ctx", "grp", None),
    )
    return jax.shard_map(
        on_device,
        mesh=mesh,
        in_specs=placed,
        out_specs=(P(("ctx", "grp"), None), P(("ctx", "grp"), None)),
        check_vma=False,
    )
```

```python
import functools

import jax
import jax.numpy as jnp
from jax import lax
from jax.experimental import pallas as pl
from jax.experimental.pallas import tpu as pltpu
from jax.sharding import PartitionSpec as P

D = 2048
HD = 128
E = 64
TOPK = 6


MESH = pl.DeviceIdType.MESH
VMEM_TOKENS = 4096


class Grid:
    def __init__(self, nz):
        ctx, grp = lax.axis_index("ctx"), lax.axis_index("grp")
        self.nz = nz
        self.z, self.x = ctx // 2, ctx % 2
        self.y, self.c = grp // 2, grp % 2
        self.fx, self.fy, self.fc = 1 - self.x, 1 - self.y, 1 - self.c

    def turn(self, dz):
        return lax.rem(self.z + dz, self.nz)

    def meet(self):
        barrier = pltpu.get_barrier_semaphore()
        partners = [device(self.turn(dz), self.x, self.y, self.c) for dz in range(1, self.nz)]
        partners += [
            device(self.z, self.fx, self.y, self.c),
            device(self.z, self.x, self.fy, self.c),
            device(self.z, self.x, self.y, self.fc),
        ]
        for partner in partners:
            pl.semaphore_signal(barrier, inc=1, device_id=partner, device_id_type=MESH)
        pl.semaphore_wait(barrier, len(partners))


def device(z, x, y, c):
    return (z * 2 + x, y * 2 + c)


def block_at(z, x, y, c):
    return (z * 2 + x) * 4 + y * 2 + c


def gather_kernel(nz, own_ref, out_ref, send_sem, recv_sem, core_sem, local_sem):
    at = Grid(nz)
    half = own_ref.shape[0] // 2
    at.meet()
    sends = []

    def send(src, dst, sem, to):
        copy = pltpu.make_async_remote_copy(
            src_ref=src,
            dst_ref=dst,
            send_sem=send_sem.at[len(sends)],
            recv_sem=sem,
            device_id=to,
            device_id_type=MESH,
        )
        copy.start()
        sends.append(copy)

    def rows_of(z, x, y, c, h):
        block = out_ref.at[block_at(z, x, y, c)]
        return block if h is None else block.at[pl.ds(h * half, half)]

    def sem_of(sems, z, x, y, h):
        return sems.at[((z * 2 + x) * 2 + y) * 2 + (0 if h is None else h)]

    def forward(z, x, y, h, to, src=None):
        ref = rows_of(z, x, y, at.c, h)
        send(ref if src is None else src, ref, sem_of(recv_sem, z, x, y, h), to)

    def forward_core(z, x, y, h, src=None):
        ref = rows_of(z, x, y, at.c, h)
        send(
            ref if src is None else src,
            ref,
            sem_of(core_sem, z, x, y, h),
            device(at.z, at.x, at.y, at.fc),
        )

    def arrive(sems, z, x, y, c, h):
        ref = rows_of(z, x, y, c, h)
        pltpu.make_async_copy(ref, ref, sem_of(sems, z, x, y, h)).wait()

    local = pltpu.make_async_copy(own_ref, out_ref.at[block_at(at.z, at.x, at.y, at.c)], local_sem)
    local.start()
    for dz in range(1, nz):
        forward(at.z, at.x, at.y, None, device(at.turn(dz), at.x, at.y, at.c), own_ref)

    to_x = device(at.z, at.fx, at.y, at.c)
    to_y = device(at.z, at.x, at.fy, at.c)

    def column(dz):
        z = at.turn(dz)
        if dz:
            arrive(recv_sem, z, at.x, at.y, at.c, None)
        src = None if dz else own_ref
        forward(z, at.x, at.y, None, to_x, src)
        forward(z, at.x, at.y, None, to_y, src)
        forward_core(z, at.x, at.y, None, src)

    def turned(dz):
        z = at.turn(dz)
        arrive(recv_sem, z, at.fx, at.y, at.c, None)
        forward(z, at.fx, at.y, 0, to_y)
        forward_core(z, at.fx, at.y, None)
        arrive(recv_sem, z, at.x, at.fy, at.c, None)
        forward(z, at.x, at.fy, 1, to_x)
        forward_core(z, at.x, at.fy, None)

    order = [0] + [d for k in range(1, nz) for d in sorted({k, nz - k}) if k <= nz - k]
    column(order[0])
    for before, now in zip(order, order[1:]):
        column(now)
        turned(before)
    turned(order[-1])
    for dz in order:
        z = at.turn(dz)
        for h in range(2):
            arrive(recv_sem, z, at.fx, at.fy, at.c, h)
            forward_core(z, at.fx, at.fy, h)
    for dz in order:
        z = at.turn(dz)
        arrive(core_sem, z, at.x, at.y, at.fc, None)
        arrive(core_sem, z, at.fx, at.y, at.fc, None)
        arrive(core_sem, z, at.x, at.fy, at.fc, None)
        arrive(core_sem, z, at.fx, at.fy, at.fc, 0)
        arrive(core_sem, z, at.fx, at.fy, at.fc, 1)
    for copy in sends:
        copy.wait_send()
    local.wait()


def gather_rows(own, nz):
    rows, width = own.shape
    blocks = nz * 8
    return pl.pallas_call(
        functools.partial(gather_kernel, nz),
        out_shape=jax.ShapeDtypeStruct((blocks, rows, width), own.dtype),
        in_specs=[pl.BlockSpec(memory_space=pltpu.VMEM)],
        out_specs=pl.BlockSpec(memory_space=pl.ANY),
        scratch_shapes=[
            pltpu.SemaphoreType.DMA((nz * 16,)),
            pltpu.SemaphoreType.DMA((nz * 8,)),
            pltpu.SemaphoreType.DMA((nz * 8,)),
            pltpu.SemaphoreType.DMA,
        ],
        compiler_params=pltpu.CompilerParams(collective_id=0, has_side_effects=True),
        name="gather_rows",
    )(own)


def combine_kernel(
    nz,
    combiner_ref,
    outs_ref,
    mix_ref,
    acc,
    core_in,
    diag_in,
    x_in,
    y_in,
    z_in,
    stage,
    stage_sem,
    send_sem,
    recv_sem,
    core_sem,
):
    at = Grid(nz)
    rows = acc.shape[1]
    half = rows // 2
    spots = [(z, x, y) for x, y in ((1, 1), (1, 0), (0, 1), (0, 0)) for z in range(1, nz + 1)]
    sends = []

    def where(spot):
        dz, dx, dy = spot
        return (
            at.turn(dz % nz),
            at.fx if dx else at.x,
            at.fy if dy else at.y,
        )

    def place(z, x, y):
        return (z * 2 + x) * 2 + y

    ahead = 3
    turns = [(spot, at.fc) for spot in spots[:ahead]]
    for i, spot in enumerate(spots):
        turns.append((spot, at.c))
        if i + ahead < len(spots):
            turns.append((spots[i + ahead], at.fc))

    def load(i):
        spot, c = turns[i]
        return pltpu.make_async_copy(
            outs_ref.at[block_at(*where(spot), c)], stage.at[i % 3], stage_sem.at[i % 3]
        )

    load(0).start()
    load(1).start()
    at.meet()

    def send(src, dst, sem, to):
        copy = pltpu.make_async_remote_copy(
            src_ref=src,
            dst_ref=dst,
            send_sem=send_sem.at[len(sends)],
            recv_sem=sem,
            device_id=to,
            device_id_type=MESH,
        )
        copy.start()
        sends.append(copy)

    def arrive(ref, sem):
        pltpu.make_async_copy(ref, ref, sem).wait()

    def make(i):
        if i + 2 < len(turns):
            load(i + 2).start()
        load(i).wait()
        spot, c = turns[i]
        block = block_at(*where(spot), c)
        slot = i % 3

        @pl.loop(0, acc.shape[2] // 512)
        def _(k):
            cols = pl.ds(pl.multiple_of(k * 512, 512), 512)
            acc[block, :, cols] = jnp.dot(
                combiner_ref[block], stage[slot, :, cols], preferred_element_type=jnp.float32
            ).astype(acc.dtype)

        return block

    def add(block, h, others):
        first, count = (0, rows) if h is None else (h * half, half)

        @pl.loop(0, count // 16)
        def _(k):
            at_acc = pl.ds(pl.multiple_of(first + k * 16, 16), 16)
            total = acc[block, at_acc, :].astype(jnp.float32)
            for ref, lead in others:
                total = total + ref[lead, at_acc, :].astype(jnp.float32)
            acc[block, at_acc, :] = total.astype(acc.dtype)

    to_x = device(at.z, at.fx, at.y, at.c)
    to_y = device(at.z, at.x, at.fy, at.c)
    to_core = device(at.z, at.x, at.y, at.fc)
    made = 0

    def give(i):
        spare = place(*where(spots[i]))
        theirs = make(made)
        send(acc.at[theirs], core_in.at[spare], core_sem.at[spare], to_core)

    for i in range(ahead):
        give(i)
        made += 1
    for i, spot in enumerate(spots):
        dz, dx, dy = spot
        z, x, y = where(spot)
        spare = place(z, x, y)
        mine = make(made)
        made += 1
        if i + ahead < len(spots):
            give(i + ahead)
            made += 1
        arrive(core_in.at[spare], core_sem.at[spare])
        if dx and dy:
            add(mine, None, [(core_in, spare)])
            send(
                acc.at[mine, pl.ds(0, half)],
                diag_in.at[z, pl.ds(0, half)],
                recv_sem.at[z],
                to_y,
            )
            send(
                acc.at[mine, pl.ds(half, half)],
                diag_in.at[z, pl.ds(half, half)],
                recv_sem.at[nz + z],
                to_x,
            )
        elif dx:
            arrive(diag_in.at[z, pl.ds(0, half)], recv_sem.at[z])
            add(mine, 0, [(core_in, spare), (diag_in, z)])
            add(mine, 1, [(core_in, spare)])
            send(acc.at[mine], x_in.at[z], recv_sem.at[2 * nz + z], to_x)
        elif dy:
            arrive(diag_in.at[z, pl.ds(half, half)], recv_sem.at[nz + z])
            add(mine, 0, [(core_in, spare)])
            add(mine, 1, [(core_in, spare), (diag_in, z)])
            send(acc.at[mine], y_in.at[z], recv_sem.at[3 * nz + z], to_y)
        else:
            arrive(x_in.at[z], recv_sem.at[2 * nz + z])
            arrive(y_in.at[z], recv_sem.at[3 * nz + z])
            add(mine, None, [(core_in, spare), (x_in, z), (y_in, z)])
            if dz % nz:
                send(
                    acc.at[mine],
                    z_in.at[at.z],
                    recv_sem.at[4 * nz + at.z],
                    device(z, at.x, at.y, at.c),
                )
    others = [at.turn(dz) for dz in range(1, nz)]
    for z in others:
        arrive(z_in.at[z], recv_sem.at[4 * nz + z])
    own = block_at(at.z, at.x, at.y, at.c)

    @pl.loop(0, rows // 16)
    def _(k):
        part = pl.ds(pl.multiple_of(k * 16, 16), 16)
        total = acc[own, part, :].astype(jnp.float32)
        for z in others:
            total = total + z_in[z, part, :].astype(jnp.float32)
        mix_ref[part, :] = total

    for copy in sends:
        copy.wait_send()


def combine_rows(combiner, outs, nz):
    blocks, rows, slots = combiner.shape
    width = outs.shape[2]
    kind = outs.dtype
    return pl.pallas_call(
        functools.partial(combine_kernel, nz),
        out_shape=jax.ShapeDtypeStruct((rows, width), jnp.float32),
        in_specs=[pl.BlockSpec(memory_space=pltpu.VMEM), pl.BlockSpec(memory_space=pl.ANY)],
        out_specs=pl.BlockSpec(memory_space=pltpu.VMEM),
        scratch_shapes=[
            pltpu.VMEM((blocks, rows, width), kind),
            pltpu.VMEM((blocks // 2, rows, width), kind),
            pltpu.VMEM((nz, rows, width), kind),
            pltpu.VMEM((nz, rows, width), kind),
            pltpu.VMEM((nz, rows, width), kind),
            pltpu.VMEM((nz, rows, width), kind),
            pltpu.VMEM((3, slots, width), kind),
            pltpu.SemaphoreType.DMA((3,)),
            pltpu.SemaphoreType.DMA((nz * 10,)),
            pltpu.SemaphoreType.DMA((nz * 5,)),
            pltpu.SemaphoreType.DMA((nz * 4,)),
        ],
        compiler_params=pltpu.CompilerParams(
            collective_id=1, has_side_effects=True, vmem_limit_bytes=56 * 1024 * 1024
        ),
        name="combine_rows",
    )(combiner, outs)


def share_kernel(
    nz, route_ref, state_ref, routes_ref, states_ref, send_sem, z_sem, x_sem, small_sem, far_sem
):
    at = Grid(nz)
    routes_ref[at.z, at.x, at.y, at.c] = route_ref[...]
    states_ref[at.z, at.x] = state_ref[...]
    at.meet()
    sends = []

    def send(ref, sem, to):
        copy = pltpu.make_async_remote_copy(
            src_ref=ref,
            dst_ref=ref,
            send_sem=send_sem.at[len(sends)],
            recv_sem=sem,
            device_id=to,
            device_id_type=MESH,
        )
        copy.start()
        sends.append(copy)

    def arrive(ref, sem):
        pltpu.make_async_copy(ref, ref, sem).wait()

    to_x = device(at.z, at.fx, at.y, at.c)
    to_y = device(at.z, at.x, at.fy, at.c)
    to_core = device(at.z, at.x, at.y, at.fc)
    send(routes_ref.at[at.z, at.x, at.y, at.c], small_sem.at[0], to_x)
    send(states_ref.at[at.z, at.x], x_sem.at[at.z], to_x)
    for dz in range(1, nz):
        send(
            states_ref.at[at.z, at.x], z_sem.at[at.z], device(at.turn(dz), at.x, at.y, at.c)
        )
    arrive(routes_ref.at[at.z, at.fx, at.y, at.c], small_sem.at[0])
    send(routes_ref.at[at.z, :, at.y, at.c], small_sem.at[1], to_y)
    arrive(routes_ref.at[at.z, :, at.fy, at.c], small_sem.at[1])
    send(routes_ref.at[at.z, :, :, at.c], small_sem.at[2], to_core)
    arrive(routes_ref.at[at.z, :, :, at.fc], small_sem.at[2])
    for dz in range(1, nz):
        send(routes_ref.at[at.z], far_sem.at[at.z], device(at.turn(dz), at.x, at.y, at.c))
    for dz in range(1, nz):
        z = at.turn(dz)
        arrive(states_ref.at[z, at.x], z_sem.at[z])
        send(states_ref.at[z, at.x], x_sem.at[z], to_x)
    for dz in range(nz):
        z = at.turn(dz)
        arrive(states_ref.at[z, at.fx], x_sem.at[z])
        if dz:
            arrive(routes_ref.at[z], far_sem.at[z])
    for copy in sends:
        copy.wait_send()


def share(route, state, nz):
    routes, states = pl.pallas_call(
        functools.partial(share_kernel, nz),
        out_shape=(
            jax.ShapeDtypeStruct((nz, 2, 2, 2) + route.shape, route.dtype),
            jax.ShapeDtypeStruct((nz, 2) + state.shape, state.dtype),
        ),
        in_specs=[pl.BlockSpec(memory_space=pltpu.VMEM)] * 2,
        out_specs=(pl.BlockSpec(memory_space=pltpu.VMEM),) * 2,
        scratch_shapes=[
            pltpu.SemaphoreType.DMA((3 * nz + 4,)),
            pltpu.SemaphoreType.DMA((nz,)),
            pltpu.SemaphoreType.DMA((nz,)),
            pltpu.SemaphoreType.DMA((3,)),
            pltpu.SemaphoreType.DMA((nz,)),
        ],
        compiler_params=pltpu.CompilerParams(collective_id=2, has_side_effects=True),
        name="share",
    )(route, state)
    return routes.reshape((nz * 8,) + route.shape), states.reshape((nz * 2,) + state.shape)


def expert_kernel(
    waves, slots, first_ref, rows_ref, routes_ref, gate_ref, up_ref, down_ref, out_ref, mix_ref, x_ref
):
    step = pl.program_id(0)
    experts = x_ref.shape[0]
    count, rows = rows_ref.shape[0], rows_ref.shape[1]

    @pl.when(step < waves)
    def _():
        row = lax.broadcasted_iota(jnp.int32, (rows, rows), 0)
        col = lax.broadcasted_iota(jnp.int32, (rows, rows), 1)
        before = (row < col).astype(jnp.bfloat16)
        own = (
            lax.broadcasted_iota(jnp.int32, (experts, rows), 0) + first_ref[0] * experts
        ).astype(jnp.float32)
        spot = lax.broadcasted_iota(jnp.int32, (experts, slots, rows), 1).astype(jnp.float32)
        for b in range(count):
            info = routes_ref[b].astype(jnp.float32)
            hits = jnp.zeros((experts, rows), jnp.float32)
            gates = jnp.zeros((experts, rows), jnp.float32)
            for k in range(TOPK):
                same = info[k : k + 1, :] == own
                hits = jnp.where(same, 1.0, hits)
                gates = jnp.where(same, info[TOPK + k : TOPK + k + 1, :], gates)
            slot = jnp.dot(hits.astype(jnp.bfloat16), before, preferred_element_type=jnp.float32)
            slot = jnp.where(hits > 0, slot, -1.0)
            placed = jnp.where(slot[:, None, :] == spot, 1.0, 0.0)
            weighed = (placed * gates[:, None, :]).reshape(experts * slots, rows)
            mix_ref[b] = weighed.T.astype(jnp.bfloat16)
            placed = placed.reshape(experts * slots, rows).astype(jnp.bfloat16)
            picked = jnp.dot(placed, rows_ref[b], preferred_element_type=jnp.float32)
            picked = picked.astype(jnp.bfloat16)
            start = pl.multiple_of((step * count + b) * slots, slots)
            for e in range(experts):
                x_ref[e, pl.ds(start, slots), :] = picked[e * slots : (e + 1) * slots]

    @pl.when(step >= waves)
    def _():
        e = step - waves
        total = x_ref.shape[1]
        part = min(total, 256)
        for p in range(0, total, part):
            x = x_ref[e, p : p + part, :]
            gate = jnp.dot(x, gate_ref[0], preferred_element_type=jnp.float32)
            up = jnp.dot(x, up_ref[0], preferred_element_type=jnp.float32)
            hidden = (jax.nn.silu(gate) * up).astype(jnp.bfloat16)
            made = jnp.dot(hidden, down_ref[0], preferred_element_type=jnp.float32)
            out_ref[p // slots : (p + part) // slots, 0] = made.astype(jnp.bfloat16).reshape(
                part // slots, slots, made.shape[1]
            )


def run_experts(all_rows, routes, gate_proj, up_proj, down_proj, slots):
    blocks, rows, width = all_rows.shape
    experts, _, units = gate_proj.shape
    count = 4
    waves = blocks // count
    first = lax.axis_index("ctx").astype(jnp.int32).reshape(1)
    wave = lambda i: (jnp.minimum(i, waves - 1), 0, 0)
    turn = lambda i: (jnp.maximum(i - waves, 0), 0, 0)
    out, mix = pl.pallas_call(
        functools.partial(expert_kernel, waves, slots),
        grid=(waves + experts,),
        out_shape=(
            jax.ShapeDtypeStruct((blocks, experts, slots, width), jnp.bfloat16),
            jax.ShapeDtypeStruct((blocks, rows, experts * slots), jnp.bfloat16),
        ),
        in_specs=[
            pl.BlockSpec(memory_space=pltpu.SMEM),
            pl.BlockSpec((count, rows, width), wave),
            pl.BlockSpec((count,) + routes.shape[1:], wave),
            pl.BlockSpec((1, width, units), turn),
            pl.BlockSpec((1, width, units), turn),
            pl.BlockSpec((1, units, width), turn),
        ],
        out_specs=(
            pl.BlockSpec((blocks, 1, slots, width), lambda i: (0, jnp.maximum(i - waves, 0), 0, 0)),
            pl.BlockSpec((count, rows, experts * slots), wave),
        ),
        scratch_shapes=[pltpu.VMEM((experts, blocks * slots, width), jnp.bfloat16)],
        compiler_params=pltpu.CompilerParams(
            dimension_semantics=("arbitrary",), vmem_limit_bytes=56 * 1024 * 1024
        ),
        name="run_experts",
    )(first, all_rows, routes, gate_proj, up_proj, down_proj)
    return out.reshape(blocks, experts * slots, width), mix


def pack_route(expert_ids, gate_weights):
    info = jnp.concatenate([expert_ids.astype(jnp.bfloat16), gate_weights.astype(jnp.bfloat16)], 1)
    return jnp.pad(info.T, ((0, 16 - 2 * TOPK), (0, 0)))


def pack_state(total, state, norm):
    high = total.astype(jnp.bfloat16)
    low = (total - high.astype(jnp.float32)).astype(jnp.bfloat16)
    wide = lambda one: jnp.broadcast_to(one[:, None, None], (one.shape[0], 1, HD))
    packed = jnp.concatenate(
        [state.astype(jnp.bfloat16), norm.astype(jnp.bfloat16)[:, None], wide(high), wide(low)], 1
    )
    return jnp.pad(packed, ((0, 0), (0, 13), (0, 0)))


def prior_of(packs):
    count, index = packs.shape[0], lax.axis_index("ctx")
    totals = packs[:, :, HD + 1, 0].astype(jnp.float32) + packs[:, :, HD + 2, 0].astype(jnp.float32)
    of = jnp.arange(count)
    between = (of[None, :] > of[:, None]) & (of[None, :] < index)
    spans = jnp.sum(jnp.where(between[:, :, None], totals[None], 0.0), axis=1)
    factor = jnp.where((of < index)[:, None], jnp.exp(spans), 0.0)
    prior = jnp.sum(factor[:, :, None, None] * packs[:, :, : HD + 1].astype(jnp.float32), axis=0)
    return prior[:, :HD], prior[:, HD]


def feature_map(values):
    return (jax.nn.elu(values.astype(jnp.float32)) + 1.0).astype(jnp.bfloat16)


def summarize(feat_key, value_rows, log_decay):
    cumulative = jnp.cumsum(log_decay, axis=1)
    block_total = cumulative[:, -1]
    trailing_keys = (
        feat_key.astype(jnp.float32) * jnp.exp(block_total[:, None] - cumulative).T[:, :, None]
    )
    shard_state = jnp.einsum(
        "jfi,jfx->fix",
        trailing_keys.astype(jnp.bfloat16),
        value_rows,
        preferred_element_type=jnp.float32,
    )
    local_norm = jnp.sum(trailing_keys, axis=0)
    return (cumulative, block_total, shard_state, local_norm)


def block_output(feat_query, feat_key, value_rows, cumulative, preceding_state, prior_norm):
    length = feat_query.shape[0]
    scores = jnp.einsum("thd,shd->hts", feat_query, feat_key, preferred_element_type=jnp.float32)
    row_index = lax.broadcasted_iota(jnp.int32, (length, length), 0)
    col_index = lax.broadcasted_iota(jnp.int32, (length, length), 1)
    causal = (col_index <= row_index)[None]
    spread = cumulative[:, :, None] - cumulative[:, None, :]
    weights = jnp.where(causal, scores * jnp.exp(jnp.where(causal, spread, 0.0)), 0.0)
    inner_den = jnp.sum(weights, axis=2).T
    inner_num = jnp.einsum(
        "hts,shd->thd", weights.astype(jnp.bfloat16), value_rows, preferred_element_type=jnp.float32
    )
    query_damping = feat_query.astype(jnp.float32) * jnp.exp(cumulative).T[:, :, None]
    outer_numerator = jnp.einsum(
        "cnm,nmp->cnp", query_damping, preceding_state, precision=lax.Precision.HIGHEST
    )
    outer_den = jnp.einsum("thk,hk->th", query_damping, prior_norm, precision=lax.Precision.HIGHEST)
    mixed_rows = ((inner_num + outer_numerator) / (inner_den + outer_den)[:, :, None]).astype(
        jnp.bfloat16
    )
    return mixed_rows.reshape(length, -1)


def local_routes(expert_ids, gate_weights, row_count, local_experts, capacity):
    blocks = expert_ids.shape[0] // row_count
    own = lax.axis_index("ctx") * local_experts + jnp.arange(local_experts, dtype=jnp.int32)
    named = (expert_ids[:, :, None] == own).astype(jnp.float32)
    gates = jnp.sum(named * gate_weights.astype(jnp.float32)[:, :, None], axis=1)
    hits = jnp.sum(named, axis=1).reshape(blocks, row_count, local_experts)
    row = lax.broadcasted_iota(jnp.int32, (row_count, row_count), 0)
    col = lax.broadcasted_iota(jnp.int32, (row_count, row_count), 1)
    before = (col < row).astype(jnp.bfloat16)
    slot = jnp.einsum(
        "rs,bse->bre", before, hits.astype(jnp.bfloat16), preferred_element_type=jnp.float32
    )
    placed = jnp.where(
        (slot[:, :, :, None] == jnp.arange(capacity, dtype=jnp.float32)) & (hits[:, :, :, None] > 0),
        1.0,
        0.0,
    )
    combiner = placed * gates.reshape(blocks, row_count, local_experts, 1)
    flat = (blocks, row_count, local_experts * capacity)
    return placed.astype(jnp.bfloat16).reshape(flat), combiner.astype(jnp.bfloat16).reshape(flat)


def on_device(
    query_heads,
    key_heads,
    value_heads,
    log_decay,
    residual,
    out_weight,
    norm_gain,
    expert_ids,
    gate_weights,
    gate_proj,
    up_proj,
    down_proj,
):
    length = query_heads.shape[0]
    local_heads = query_heads.shape[1] // HD
    feat_query = feature_map(query_heads).reshape(length, local_heads, HD)
    feat_key = feature_map(key_heads).reshape(length, local_heads, HD)
    value_rows = value_heads.reshape(length, local_heads, HD)
    cumulative, block_total, shard_state, local_norm = summarize(feat_key, value_rows, log_decay)
    row_count = expert_ids.shape[0]
    blocks = lax.axis_size("ctx") * lax.axis_size("grp")
    nz = lax.axis_size("ctx") // 2
    everyone = ("ctx", "grp")
    kernels = lax.axis_size("grp") == 4 and nz > 1 and blocks * row_count <= VMEM_TOKENS
    packed = pack_state(block_total, shard_state, local_norm)
    if kernels:
        routes, packs = share(pack_route(expert_ids, gate_weights), packed, nz)
    else:
        packs = lax.all_gather(packed, "ctx")
    preceding_state, prior_norm = prior_of(packs)
    mixed_rows = block_output(
        feat_query, feat_key, value_rows, cumulative, preceding_state, prior_norm
    )
    head_rows = lax.all_to_all(mixed_rows, "grp", split_axis=0, concat_axis=1, tiled=True)
    projected = jnp.dot(head_rows, out_weight, preferred_element_type=jnp.float32)
    attended = (residual.astype(jnp.float32) + projected).astype(jnp.bfloat16)
    widened = attended.astype(jnp.float32)
    normed = (
        widened * lax.rsqrt(jnp.mean(widened * widened, axis=1, keepdims=True) + 1e-06) * norm_gain
    ).astype(jnp.bfloat16)
    local_experts = gate_proj.shape[0]
    capacity = (5 * row_count * TOPK + 4 * E - 1) // (4 * E)
    capacity = (capacity + 15) // 16 * 16
    if kernels:
        all_rows = gather_rows(normed, nz)
        partial_rows, combiner = run_experts(
            all_rows, routes, gate_proj, up_proj, down_proj, capacity
        )
        expert_mix = combine_rows(combiner, partial_rows, nz)
    else:
        all_ids = lax.all_gather(expert_ids, everyone, axis=0, tiled=True)
        all_gates = lax.all_gather(gate_weights.astype(jnp.bfloat16), everyone, axis=0, tiled=True)
        placed, combiner = local_routes(all_ids, all_gates, row_count, local_experts, capacity)
        all_rows = lax.all_gather(normed, everyone, axis=0, tiled=True)
        block_rows = jnp.einsum(
            "brs,brd->bsd",
            placed,
            all_rows.reshape(blocks, row_count, D),
            preferred_element_type=jnp.float32,
        ).astype(jnp.bfloat16).reshape(blocks, local_experts, capacity, D)
        gate_part = jnp.einsum(
            "secd,edf->secf", block_rows, gate_proj, preferred_element_type=jnp.float32
        )
        up_part = jnp.einsum(
            "secd,edf->secf", block_rows, up_proj, preferred_element_type=jnp.float32
        )
        hidden = (jax.nn.silu(gate_part) * up_part).astype(jnp.bfloat16)
        partial_out = jnp.einsum(
            "secf,efd->secd", hidden, down_proj, preferred_element_type=jnp.float32
        ).astype(jnp.bfloat16)
        partial_mix = jnp.einsum(
            "brs,bsd->brd",
            combiner,
            partial_out.reshape(blocks, local_experts * capacity, D),
            preferred_element_type=jnp.float32,
        ).astype(jnp.bfloat16)
        expert_mix = lax.psum_scatter(
            partial_mix.reshape(-1, D), everyone, scatter_dimension=0, tiled=True
        ).astype(jnp.float32)
    layer_out = (widened + expert_mix).astype(jnp.bfloat16)
    return (attended, layer_out)


def solution(mesh):
    placed = (
        P("ctx", "grp"),
        P("ctx", "grp"),
        P("ctx", "grp"),
        P("grp", "ctx"),
        P(("ctx", "grp"), None),
        P(),
        P(),
        P(("ctx", "grp"), None),
        P(("ctx", "grp"), None),
        P("ctx", None, "grp"),
        P("ctx", None, "grp"),
        P("ctx", "grp", None),
    )
    return jax.shard_map(
        on_device,
        mesh=mesh,
        in_specs=placed,
        out_specs=(P(("ctx", "grp"), None), P(("ctx", "grp"), None)),
        check_vma=False,
    )
```

```python
import functools

import jax
import jax.numpy as jnp
from jax import lax
from jax.experimental import pallas as pl
from jax.experimental.pallas import tpu as pltpu
from jax.sharding import PartitionSpec as P

D = 2048
HD = 128
E = 64
TOPK = 6


MESH = pl.DeviceIdType.MESH
VMEM_TOKENS = 4096


class Grid:
    def __init__(self, nz):
        ctx, grp = lax.axis_index("ctx"), lax.axis_index("grp")
        self.nz = nz
        self.z, self.x = ctx // 2, ctx % 2
        self.y, self.c = grp // 2, grp % 2
        self.fx, self.fy, self.fc = 1 - self.x, 1 - self.y, 1 - self.c

    def turn(self, dz):
        return lax.rem(self.z + dz, self.nz)

    def meet(self):
        barrier = pltpu.get_barrier_semaphore()
        partners = [device(self.turn(dz), self.x, self.y, self.c) for dz in range(1, self.nz)]
        partners += [
            device(self.z, self.fx, self.y, self.c),
            device(self.z, self.x, self.fy, self.c),
            device(self.z, self.x, self.y, self.fc),
        ]
        for partner in partners:
            pl.semaphore_signal(barrier, inc=1, device_id=partner, device_id_type=MESH)
        pl.semaphore_wait(barrier, len(partners))


def device(z, x, y, c):
    return (z * 2 + x, y * 2 + c)


def block_at(z, x, y, c):
    return (z * 2 + x) * 4 + y * 2 + c


def gather_kernel(nz, own_ref, out_ref, send_sem, recv_sem, core_sem, local_sem):
    at = Grid(nz)
    half = own_ref.shape[0] // 2
    at.meet()
    sends = []

    def send(src, dst, sem, to, when):
        copy = pltpu.make_async_remote_copy(
            src_ref=src,
            dst_ref=dst,
            send_sem=send_sem.at[len(sends)],
            recv_sem=sem,
            device_id=to,
            device_id_type=MESH,
        )
        sends.append((when, copy))
        if when is None:
            copy.start()
        else:
            pl.when(when)(copy.start)

    def rows_of(z, x, y, c, h):
        block = out_ref.at[block_at(z, x, y, c)]
        return block if h is None else block.at[pl.ds(h * half, half)]

    def sem_of(sems, z, x, y, h):
        return sems.at[((z * 2 + x) * 2 + y) * 2 + (0 if h is None else h)]

    def forward(z, x, y, h, to, when=None, src=None):
        ref = rows_of(z, x, y, at.c, h)
        send(ref if src is None else src, ref, sem_of(recv_sem, z, x, y, h), to, when)

    def forward_core(z, x, y, h, src=None):
        ref = rows_of(z, x, y, at.c, h)
        to = device(at.z, at.x, at.y, at.fc)
        send(ref if src is None else src, ref, sem_of(core_sem, z, x, y, h), to, None)

    def arrive(sems, z, x, y, c, h):
        ref = rows_of(z, x, y, c, h)
        pltpu.make_async_copy(ref, ref, sem_of(sems, z, x, y, h)).wait()

    local = pltpu.make_async_copy(own_ref, out_ref.at[block_at(at.z, at.x, at.y, at.c)], local_sem)
    local.start()
    to_x = device(at.z, at.fx, at.y, at.c)
    to_y = device(at.z, at.x, at.fy, at.c)
    to_up = device(jnp.minimum(at.z + 1, nz - 1), at.x, at.y, at.c)
    to_down = device(jnp.maximum(at.z - 1, 0), at.x, at.y, at.c)
    more_up, more_down = at.z < nz - 1, at.z > 0

    def spread(z, src=None):
        forward(z, at.x, at.y, None, to_x, None, src)
        forward(z, at.x, at.y, None, to_y, None, src)
        forward_core(z, at.x, at.y, None, src)

    forward(at.z, at.x, at.y, None, to_up, more_up, own_ref)
    forward(at.z, at.x, at.y, None, to_down, more_down, own_ref)
    spread(at.z, own_ref)

    def nearest(k):
        reach = jnp.minimum(at.z, nz - 1 - at.z)
        both = k < 2 * reach
        far = k - reach + 1
        low = jnp.where(both, k % 2 == 0, at.z > reach)
        distance = jnp.where(both, k // 2 + 1, far)
        return jnp.where(low, at.z - distance, at.z + distance), low

    def column(k):
        z, low = nearest(k)
        arrive(recv_sem, z, at.x, at.y, at.c, None)
        forward(z, at.x, at.y, None, to_up, low & more_up)
        forward(z, at.x, at.y, None, to_down, jnp.logical_not(low) & more_down)
        spread(z)

    def turned(z):
        arrive(recv_sem, z, at.fx, at.y, at.c, None)
        forward(z, at.fx, at.y, 0, to_y)
        forward_core(z, at.fx, at.y, None)
        arrive(recv_sem, z, at.x, at.fy, at.c, None)
        forward(z, at.x, at.fy, 1, to_x)
        forward_core(z, at.x, at.fy, None)

    column(0)
    turned(at.z)
    for k in range(1, nz - 1):
        column(k)
    for k in range(nz - 1):
        turned(nearest(k)[0])
    order = [at.z] + [nearest(k)[0] for k in range(nz - 1)]
    for z in order:
        for h in range(2):
            arrive(recv_sem, z, at.fx, at.fy, at.c, h)
            forward_core(z, at.fx, at.fy, h)
    for z in order:
        arrive(core_sem, z, at.x, at.y, at.fc, None)
        arrive(core_sem, z, at.fx, at.y, at.fc, None)
        arrive(core_sem, z, at.x, at.fy, at.fc, None)
        arrive(core_sem, z, at.fx, at.fy, at.fc, 0)
        arrive(core_sem, z, at.fx, at.fy, at.fc, 1)
    for when, copy in sends:
        if when is None:
            copy.wait_send()
        else:
            pl.when(when)(copy.wait_send)
    local.wait()


def gather_rows(own, nz):
    rows, width = own.shape
    blocks = nz * 8
    return pl.pallas_call(
        functools.partial(gather_kernel, nz),
        out_shape=jax.ShapeDtypeStruct((blocks, rows, width), own.dtype),
        in_specs=[pl.BlockSpec(memory_space=pltpu.VMEM)],
        out_specs=pl.BlockSpec(memory_space=pl.ANY),
        scratch_shapes=[
            pltpu.SemaphoreType.DMA((nz * 16,)),
            pltpu.SemaphoreType.DMA((nz * 8,)),
            pltpu.SemaphoreType.DMA((nz * 8,)),
            pltpu.SemaphoreType.DMA,
        ],
        compiler_params=pltpu.CompilerParams(collective_id=0, has_side_effects=True),
        name="gather_rows",
    )(own)


def combine_kernel(
    nz,
    combiner_ref,
    outs_ref,
    mix_ref,
    acc,
    core_in,
    diag_in,
    x_in,
    y_in,
    z_in,
    stage,
    stage_sem,
    send_sem,
    recv_sem,
    core_sem,
):
    at = Grid(nz)
    rows = acc.shape[1]
    half = rows // 2
    lead = 1
    spots = []
    for z in range(1, nz + 2 * lead + 1):
        spots += [(z, 1, 1)] if z <= nz else []
        spots += [(z - lead, 1, 0), (z - lead, 0, 1)] if 1 <= z - lead <= nz else []
        spots += [(z - 2 * lead, 0, 0)] if z > 2 * lead else []
    sends = []

    def where(spot):
        dz, dx, dy = spot
        return (
            at.turn(dz % nz),
            at.fx if dx else at.x,
            at.fy if dy else at.y,
        )

    def place(z, x, y):
        return (z * 2 + x) * 2 + y

    ahead = 3
    turns = [(spot, at.fc) for spot in spots[:ahead]]
    for i, spot in enumerate(spots):
        turns.append((spot, at.c))
        if i + ahead < len(spots):
            turns.append((spots[i + ahead], at.fc))

    def load(i):
        spot, c = turns[i]
        return pltpu.make_async_copy(
            outs_ref.at[block_at(*where(spot), c)], stage.at[i % 3], stage_sem.at[i % 3]
        )

    load(0).start()
    load(1).start()
    at.meet()

    def send(src, dst, sem, to):
        copy = pltpu.make_async_remote_copy(
            src_ref=src,
            dst_ref=dst,
            send_sem=send_sem.at[len(sends)],
            recv_sem=sem,
            device_id=to,
            device_id_type=MESH,
        )
        copy.start()
        sends.append(copy)

    def arrive(ref, sem):
        pltpu.make_async_copy(ref, ref, sem).wait()

    def make(i):
        if i + 2 < len(turns):
            load(i + 2).start()
        load(i).wait()
        spot, c = turns[i]
        block = block_at(*where(spot), c)
        slot = i % 3

        @pl.loop(0, acc.shape[2] // 512)
        def _(k):
            cols = pl.ds(pl.multiple_of(k * 512, 512), 512)
            acc[block, :, cols] = jnp.dot(
                combiner_ref[block], stage[slot, :, cols], preferred_element_type=jnp.float32
            ).astype(acc.dtype)

        return block

    def add(block, h, others):
        first, count = (0, rows) if h is None else (h * half, half)

        @pl.loop(0, count // 16)
        def _(k):
            at_acc = pl.ds(pl.multiple_of(first + k * 16, 16), 16)
            total = acc[block, at_acc, :].astype(jnp.float32)
            for ref, lead in others:
                total = total + ref[lead, at_acc, :].astype(jnp.float32)
            acc[block, at_acc, :] = total.astype(acc.dtype)

    to_x = device(at.z, at.fx, at.y, at.c)
    to_y = device(at.z, at.x, at.fy, at.c)
    to_core = device(at.z, at.x, at.y, at.fc)
    made = 0

    def give(i):
        spare = place(*where(spots[i]))
        theirs = make(made)
        send(acc.at[theirs], core_in.at[spare], core_sem.at[spare], to_core)

    for i in range(ahead):
        give(i)
        made += 1
    for i, spot in enumerate(spots):
        dz, dx, dy = spot
        z, x, y = where(spot)
        spare = place(z, x, y)
        mine = make(made)
        made += 1
        if i + ahead < len(spots):
            give(i + ahead)
            made += 1
        arrive(core_in.at[spare], core_sem.at[spare])
        if dx and dy:
            add(mine, None, [(core_in, spare)])
            send(
                acc.at[mine, pl.ds(0, half)],
                diag_in.at[z, pl.ds(0, half)],
                recv_sem.at[z],
                to_y,
            )
            send(
                acc.at[mine, pl.ds(half, half)],
                diag_in.at[z, pl.ds(half, half)],
                recv_sem.at[nz + z],
                to_x,
            )
        elif dx:
            arrive(diag_in.at[z, pl.ds(0, half)], recv_sem.at[z])
            add(mine, 0, [(core_in, spare), (diag_in, z)])
            add(mine, 1, [(core_in, spare)])
            send(acc.at[mine], x_in.at[z], recv_sem.at[2 * nz + z], to_x)
        elif dy:
            arrive(diag_in.at[z, pl.ds(half, half)], recv_sem.at[nz + z])
            add(mine, 0, [(core_in, spare)])
            add(mine, 1, [(core_in, spare), (diag_in, z)])
            send(acc.at[mine], y_in.at[z], recv_sem.at[3 * nz + z], to_y)
        else:
            arrive(x_in.at[z], recv_sem.at[2 * nz + z])
            arrive(y_in.at[z], recv_sem.at[3 * nz + z])
            add(mine, None, [(core_in, spare), (x_in, z), (y_in, z)])
            if dz % nz:
                send(
                    acc.at[mine],
                    z_in.at[at.z],
                    recv_sem.at[4 * nz + at.z],
                    device(z, at.x, at.y, at.c),
                )
    others = [at.turn(dz) for dz in range(1, nz)]
    for z in others:
        arrive(z_in.at[z], recv_sem.at[4 * nz + z])
    own = block_at(at.z, at.x, at.y, at.c)

    @pl.loop(0, rows // 16)
    def _(k):
        part = pl.ds(pl.multiple_of(k * 16, 16), 16)
        total = acc[own, part, :].astype(jnp.float32)
        for z in others:
            total = total + z_in[z, part, :].astype(jnp.float32)
        mix_ref[part, :] = total

    for copy in sends:
        copy.wait_send()


def combine_rows(combiner, outs, nz):
    blocks, rows, slots = combiner.shape
    width = outs.shape[2]
    kind = outs.dtype
    return pl.pallas_call(
        functools.partial(combine_kernel, nz),
        out_shape=jax.ShapeDtypeStruct((rows, width), jnp.float32),
        in_specs=[pl.BlockSpec(memory_space=pltpu.VMEM), pl.BlockSpec(memory_space=pl.ANY)],
        out_specs=pl.BlockSpec(memory_space=pltpu.VMEM),
        scratch_shapes=[
            pltpu.VMEM((blocks, rows, width), kind),
            pltpu.VMEM((blocks // 2, rows, width), kind),
            pltpu.VMEM((nz, rows, width), kind),
            pltpu.VMEM((nz, rows, width), kind),
            pltpu.VMEM((nz, rows, width), kind),
            pltpu.VMEM((nz, rows, width), kind),
            pltpu.VMEM((3, slots, width), kind),
            pltpu.SemaphoreType.DMA((3,)),
            pltpu.SemaphoreType.DMA((nz * 10,)),
            pltpu.SemaphoreType.DMA((nz * 5,)),
            pltpu.SemaphoreType.DMA((nz * 4,)),
        ],
        compiler_params=pltpu.CompilerParams(
            collective_id=1, has_side_effects=True, vmem_limit_bytes=56 * 1024 * 1024
        ),
        name="combine_rows",
    )(combiner, outs)


def share_kernel(
    nz, route_ref, state_ref, routes_ref, states_ref, send_sem, z_sem, x_sem, small_sem, far_sem
):
    at = Grid(nz)
    routes_ref[at.z, at.x, at.y, at.c] = route_ref[...]
    states_ref[at.z, at.x] = state_ref[...]
    at.meet()
    sends = []

    def send(ref, sem, to):
        copy = pltpu.make_async_remote_copy(
            src_ref=ref,
            dst_ref=ref,
            send_sem=send_sem.at[len(sends)],
            recv_sem=sem,
            device_id=to,
            device_id_type=MESH,
        )
        copy.start()
        sends.append(copy)

    def arrive(ref, sem):
        pltpu.make_async_copy(ref, ref, sem).wait()

    to_x = device(at.z, at.fx, at.y, at.c)
    to_y = device(at.z, at.x, at.fy, at.c)
    to_core = device(at.z, at.x, at.y, at.fc)
    send(routes_ref.at[at.z, at.x, at.y, at.c], small_sem.at[0], to_x)
    send(states_ref.at[at.z, at.x], x_sem.at[at.z], to_x)
    for dz in range(1, nz):
        send(
            states_ref.at[at.z, at.x], z_sem.at[at.z], device(at.turn(dz), at.x, at.y, at.c)
        )
    arrive(routes_ref.at[at.z, at.fx, at.y, at.c], small_sem.at[0])
    send(routes_ref.at[at.z, :, at.y, at.c], small_sem.at[1], to_y)
    arrive(routes_ref.at[at.z, :, at.fy, at.c], small_sem.at[1])
    send(routes_ref.at[at.z, :, :, at.c], small_sem.at[2], to_core)
    arrive(routes_ref.at[at.z, :, :, at.fc], small_sem.at[2])
    for dz in range(1, nz):
        send(routes_ref.at[at.z], far_sem.at[at.z], device(at.turn(dz), at.x, at.y, at.c))
    for dz in range(1, nz):
        z = at.turn(dz)
        arrive(states_ref.at[z, at.x], z_sem.at[z])
        send(states_ref.at[z, at.x], x_sem.at[z], to_x)
    for dz in range(nz):
        z = at.turn(dz)
        arrive(states_ref.at[z, at.fx], x_sem.at[z])
        if dz:
            arrive(routes_ref.at[z], far_sem.at[z])
    for copy in sends:
        copy.wait_send()


def share(route, state, nz):
    routes, states = pl.pallas_call(
        functools.partial(share_kernel, nz),
        out_shape=(
            jax.ShapeDtypeStruct((nz, 2, 2, 2) + route.shape, route.dtype),
            jax.ShapeDtypeStruct((nz, 2) + state.shape, state.dtype),
        ),
        in_specs=[pl.BlockSpec(memory_space=pltpu.VMEM)] * 2,
        out_specs=(pl.BlockSpec(memory_space=pltpu.VMEM),) * 2,
        scratch_shapes=[
            pltpu.SemaphoreType.DMA((3 * nz + 4,)),
            pltpu.SemaphoreType.DMA((nz,)),
            pltpu.SemaphoreType.DMA((nz,)),
            pltpu.SemaphoreType.DMA((3,)),
            pltpu.SemaphoreType.DMA((nz,)),
        ],
        compiler_params=pltpu.CompilerParams(collective_id=2, has_side_effects=True),
        name="share",
    )(route, state)
    return routes.reshape((nz * 8,) + route.shape), states.reshape((nz * 2,) + state.shape)


def expert_kernel(
    waves, slots, first_ref, rows_ref, routes_ref, gate_ref, up_ref, down_ref, out_ref, mix_ref, x_ref
):
    step = pl.program_id(0)
    experts = x_ref.shape[0]
    count, rows = rows_ref.shape[0], rows_ref.shape[1]

    @pl.when(step < waves)
    def _():
        row = lax.broadcasted_iota(jnp.int32, (rows, rows), 0)
        col = lax.broadcasted_iota(jnp.int32, (rows, rows), 1)
        before = (row < col).astype(jnp.bfloat16)
        own = (
            lax.broadcasted_iota(jnp.int32, (experts, rows), 0) + first_ref[0] * experts
        ).astype(jnp.float32)
        spot = lax.broadcasted_iota(jnp.int32, (experts, slots, rows), 1).astype(jnp.float32)
        for b in range(count):
            info = routes_ref[b].astype(jnp.float32)
            hits = jnp.zeros((experts, rows), jnp.float32)
            gates = jnp.zeros((experts, rows), jnp.float32)
            for k in range(TOPK):
                same = info[k : k + 1, :] == own
                hits = jnp.where(same, 1.0, hits)
                gates = jnp.where(same, info[TOPK + k : TOPK + k + 1, :], gates)
            slot = jnp.dot(hits.astype(jnp.bfloat16), before, preferred_element_type=jnp.float32)
            slot = jnp.where(hits > 0, slot, -1.0)
            placed = jnp.where(slot[:, None, :] == spot, 1.0, 0.0)
            weighed = (placed * gates[:, None, :]).reshape(experts * slots, rows)
            mix_ref[b] = weighed.T.astype(jnp.bfloat16)
            placed = placed.reshape(experts * slots, rows).astype(jnp.bfloat16)
            picked = jnp.dot(placed, rows_ref[b], preferred_element_type=jnp.float32)
            picked = picked.astype(jnp.bfloat16)
            start = pl.multiple_of((step * count + b) * slots, slots)
            for e in range(experts):
                x_ref[e, pl.ds(start, slots), :] = picked[e * slots : (e + 1) * slots]

    @pl.when(step >= waves)
    def _():
        e = step - waves
        total = x_ref.shape[1]
        part = min(total, 512)
        for p in range(0, total, part):
            x = x_ref[e, p : p + part, :]
            across = (((1,), (1,)), ((), ()))
            gate = lax.dot_general(x, gate_ref[0], across, preferred_element_type=jnp.float32)
            up = lax.dot_general(x, up_ref[0], across, preferred_element_type=jnp.float32)
            hidden = (jax.nn.silu(gate) * up).astype(jnp.bfloat16)
            made = jnp.dot(hidden, down_ref[0], preferred_element_type=jnp.float32)
            out_ref[p // slots : (p + part) // slots, 0] = made.astype(jnp.bfloat16).reshape(
                part // slots, slots, made.shape[1]
            )


def run_experts(all_rows, routes, gate_proj, up_proj, down_proj, slots):
    blocks, rows, width = all_rows.shape
    experts, _, units = gate_proj.shape
    count = 4
    waves = blocks // count
    first = lax.axis_index("ctx").astype(jnp.int32).reshape(1)
    wave = lambda i: (jnp.minimum(i, waves - 1), 0, 0)
    turn = lambda i: (jnp.maximum(i - waves, 0), 0, 0)
    out, mix = pl.pallas_call(
        functools.partial(expert_kernel, waves, slots),
        grid=(waves + experts,),
        out_shape=(
            jax.ShapeDtypeStruct((blocks, experts, slots, width), jnp.bfloat16),
            jax.ShapeDtypeStruct((blocks, rows, experts * slots), jnp.bfloat16),
        ),
        in_specs=[
            pl.BlockSpec(memory_space=pltpu.SMEM),
            pl.BlockSpec((count, rows, width), wave),
            pl.BlockSpec((count,) + routes.shape[1:], wave),
            pl.BlockSpec((1, units, width), turn),
            pl.BlockSpec((1, units, width), turn),
            pl.BlockSpec((1, units, width), turn),
        ],
        out_specs=(
            pl.BlockSpec((blocks, 1, slots, width), lambda i: (0, jnp.maximum(i - waves, 0), 0, 0)),
            pl.BlockSpec((count, rows, experts * slots), wave),
        ),
        scratch_shapes=[pltpu.VMEM((experts, blocks * slots, width), jnp.bfloat16)],
        compiler_params=pltpu.CompilerParams(
            dimension_semantics=("arbitrary",), vmem_limit_bytes=56 * 1024 * 1024
        ),
        name="run_experts",
    )(
        first,
        all_rows,
        routes,
        jnp.swapaxes(gate_proj, 1, 2),
        jnp.swapaxes(up_proj, 1, 2),
        down_proj,
    )
    return out.reshape(blocks, experts * slots, width), mix


def pack_route(expert_ids, gate_weights):
    info = jnp.concatenate([expert_ids.astype(jnp.bfloat16), gate_weights.astype(jnp.bfloat16)], 1)
    return jnp.pad(info.T, ((0, 16 - 2 * TOPK), (0, 0)))


def pack_state(total, state, norm):
    high = total.astype(jnp.bfloat16)
    low = (total - high.astype(jnp.float32)).astype(jnp.bfloat16)
    wide = lambda one: jnp.broadcast_to(one[:, None, None], (one.shape[0], 1, HD))
    packed = jnp.concatenate(
        [state.astype(jnp.bfloat16), norm.astype(jnp.bfloat16)[:, None], wide(high), wide(low)], 1
    )
    return jnp.pad(packed, ((0, 0), (0, 13), (0, 0)))


def prior_of(packs):
    count, index = packs.shape[0], lax.axis_index("ctx")
    totals = packs[:, :, HD + 1, 0].astype(jnp.float32) + packs[:, :, HD + 2, 0].astype(jnp.float32)
    of = jnp.arange(count)
    between = (of[None, :] > of[:, None]) & (of[None, :] < index)
    spans = jnp.sum(jnp.where(between[:, :, None], totals[None], 0.0), axis=1)
    factor = jnp.where((of < index)[:, None], jnp.exp(spans), 0.0)
    prior = jnp.sum(factor[:, :, None, None] * packs[:, :, : HD + 1].astype(jnp.float32), axis=0)
    return prior[:, :HD], prior[:, HD]


def feature_map(values):
    return (jax.nn.elu(values.astype(jnp.float32)) + 1.0).astype(jnp.bfloat16)


def summarize(feat_key, value_rows, log_decay):
    cumulative = jnp.cumsum(log_decay, axis=1)
    block_total = cumulative[:, -1]
    trailing_keys = (
        feat_key.astype(jnp.float32) * jnp.exp(block_total[:, None] - cumulative).T[:, :, None]
    )
    shard_state = jnp.einsum(
        "jfi,jfx->fix",
        trailing_keys.astype(jnp.bfloat16),
        value_rows,
        preferred_element_type=jnp.float32,
    )
    local_norm = jnp.sum(trailing_keys, axis=0)
    return (cumulative, block_total, shard_state, local_norm)


def block_output(feat_query, feat_key, value_rows, cumulative, preceding_state, prior_norm):
    length = feat_query.shape[0]
    scores = jnp.einsum("thd,shd->hts", feat_query, feat_key, preferred_element_type=jnp.float32)
    row_index = lax.broadcasted_iota(jnp.int32, (length, length), 0)
    col_index = lax.broadcasted_iota(jnp.int32, (length, length), 1)
    causal = (col_index <= row_index)[None]
    spread = cumulative[:, :, None] - cumulative[:, None, :]
    weights = jnp.where(causal, scores * jnp.exp(jnp.where(causal, spread, 0.0)), 0.0)
    inner_den = jnp.sum(weights, axis=2).T
    inner_num = jnp.einsum(
        "hts,shd->thd", weights.astype(jnp.bfloat16), value_rows, preferred_element_type=jnp.float32
    )
    query_damping = feat_query.astype(jnp.float32) * jnp.exp(cumulative).T[:, :, None]
    outer_numerator = jnp.einsum(
        "cnm,nmp->cnp", query_damping, preceding_state, precision=lax.Precision.HIGHEST
    )
    outer_den = jnp.einsum("thk,hk->th", query_damping, prior_norm, precision=lax.Precision.HIGHEST)
    mixed_rows = ((inner_num + outer_numerator) / (inner_den + outer_den)[:, :, None]).astype(
        jnp.bfloat16
    )
    return mixed_rows.reshape(length, -1)


def local_routes(expert_ids, gate_weights, row_count, local_experts, capacity):
    blocks = expert_ids.shape[0] // row_count
    own = lax.axis_index("ctx") * local_experts + jnp.arange(local_experts, dtype=jnp.int32)
    named = (expert_ids[:, :, None] == own).astype(jnp.float32)
    gates = jnp.sum(named * gate_weights.astype(jnp.float32)[:, :, None], axis=1)
    hits = jnp.sum(named, axis=1).reshape(blocks, row_count, local_experts)
    row = lax.broadcasted_iota(jnp.int32, (row_count, row_count), 0)
    col = lax.broadcasted_iota(jnp.int32, (row_count, row_count), 1)
    before = (col < row).astype(jnp.bfloat16)
    slot = jnp.einsum(
        "rs,bse->bre", before, hits.astype(jnp.bfloat16), preferred_element_type=jnp.float32
    )
    placed = jnp.where(
        (slot[:, :, :, None] == jnp.arange(capacity, dtype=jnp.float32)) & (hits[:, :, :, None] > 0),
        1.0,
        0.0,
    )
    combiner = placed * gates.reshape(blocks, row_count, local_experts, 1)
    flat = (blocks, row_count, local_experts * capacity)
    return placed.astype(jnp.bfloat16).reshape(flat), combiner.astype(jnp.bfloat16).reshape(flat)


def on_device(
    query_heads,
    key_heads,
    value_heads,
    log_decay,
    residual,
    out_weight,
    norm_gain,
    expert_ids,
    gate_weights,
    gate_proj,
    up_proj,
    down_proj,
):
    length = query_heads.shape[0]
    local_heads = query_heads.shape[1] // HD
    feat_query = feature_map(query_heads).reshape(length, local_heads, HD)
    feat_key = feature_map(key_heads).reshape(length, local_heads, HD)
    value_rows = value_heads.reshape(length, local_heads, HD)
    cumulative, block_total, shard_state, local_norm = summarize(feat_key, value_rows, log_decay)
    row_count = expert_ids.shape[0]
    blocks = lax.axis_size("ctx") * lax.axis_size("grp")
    nz = lax.axis_size("ctx") // 2
    everyone = ("ctx", "grp")
    kernels = lax.axis_size("grp") == 4 and nz > 1 and blocks * row_count <= VMEM_TOKENS
    packed = pack_state(block_total, shard_state, local_norm)
    if kernels:
        routes, packs = share(pack_route(expert_ids, gate_weights), packed, nz)
    else:
        packs = lax.all_gather(packed, "ctx")
    preceding_state, prior_norm = prior_of(packs)
    mixed_rows = block_output(
        feat_query, feat_key, value_rows, cumulative, preceding_state, prior_norm
    )
    head_rows = lax.all_to_all(mixed_rows, "grp", split_axis=0, concat_axis=1, tiled=True)
    projected = jnp.dot(head_rows, out_weight, preferred_element_type=jnp.float32)
    attended = (residual.astype(jnp.float32) + projected).astype(jnp.bfloat16)
    widened = attended.astype(jnp.float32)
    normed = (
        widened * lax.rsqrt(jnp.mean(widened * widened, axis=1, keepdims=True) + 1e-06) * norm_gain
    ).astype(jnp.bfloat16)
    local_experts = gate_proj.shape[0]
    capacity = (5 * row_count * TOPK + 4 * E - 1) // (4 * E)
    capacity = (capacity + 15) // 16 * 16
    if kernels:
        all_rows = gather_rows(normed, nz)
        partial_rows, combiner = run_experts(
            all_rows, routes, gate_proj, up_proj, down_proj, capacity
        )
        expert_mix = combine_rows(combiner, partial_rows, nz)
    else:
        all_ids = lax.all_gather(expert_ids, everyone, axis=0, tiled=True)
        all_gates = lax.all_gather(gate_weights.astype(jnp.bfloat16), everyone, axis=0, tiled=True)
        placed, combiner = local_routes(all_ids, all_gates, row_count, local_experts, capacity)
        all_rows = lax.all_gather(normed, everyone, axis=0, tiled=True)
        block_rows = jnp.einsum(
            "brs,brd->bsd",
            placed,
            all_rows.reshape(blocks, row_count, D),
            preferred_element_type=jnp.float32,
        ).astype(jnp.bfloat16).reshape(blocks, local_experts, capacity, D)
        gate_part = jnp.einsum(
            "secd,edf->secf", block_rows, gate_proj, preferred_element_type=jnp.float32
        )
        up_part = jnp.einsum(
            "secd,edf->secf", block_rows, up_proj, preferred_element_type=jnp.float32
        )
        hidden = (jax.nn.silu(gate_part) * up_part).astype(jnp.bfloat16)
        partial_out = jnp.einsum(
            "secf,efd->secd", hidden, down_proj, preferred_element_type=jnp.float32
        ).astype(jnp.bfloat16)
        partial_mix = jnp.einsum(
            "brs,bsd->brd",
            combiner,
            partial_out.reshape(blocks, local_experts * capacity, D),
            preferred_element_type=jnp.float32,
        ).astype(jnp.bfloat16)
        expert_mix = lax.psum_scatter(
            partial_mix.reshape(-1, D), everyone, scatter_dimension=0, tiled=True
        ).astype(jnp.float32)
    layer_out = (widened + expert_mix).astype(jnp.bfloat16)
    return (attended, layer_out)


def solution(mesh):
    placed = (
        P("ctx", "grp"),
        P("ctx", "grp"),
        P("ctx", "grp"),
        P("grp", "ctx"),
        P(("ctx", "grp"), None),
        P(),
        P(),
        P(("ctx", "grp"), None),
        P(("ctx", "grp"), None),
        P("ctx", None, "grp"),
        P("ctx", None, "grp"),
        P("ctx", "grp", None),
    )
    return jax.shard_map(
        on_device,
        mesh=mesh,
        in_specs=placed,
        out_specs=(P(("ctx", "grp"), None), P(("ctx", "grp"), None)),
        check_vma=False,
    )
```

```python
import functools

import jax
import jax.numpy as jnp
from jax import lax
from jax.experimental import pallas as pl
from jax.experimental.pallas import tpu as pltpu
from jax.sharding import PartitionSpec as P

D = 2048
HD = 128
E = 64
TOPK = 6


MESH = pl.DeviceIdType.MESH
VMEM_TOKENS = 4096


class Grid:
    def __init__(self, nz):
        ctx, grp = lax.axis_index("ctx"), lax.axis_index("grp")
        self.nz = nz
        self.z, self.x = ctx // 2, ctx % 2
        self.y, self.c = grp // 2, grp % 2
        self.fx, self.fy, self.fc = 1 - self.x, 1 - self.y, 1 - self.c

    def turn(self, dz):
        return lax.rem(self.z + dz, self.nz)

    def meet(self):
        barrier = pltpu.get_barrier_semaphore()
        partners = [device(self.turn(dz), self.x, self.y, self.c) for dz in range(1, self.nz)]
        partners += [
            device(self.z, self.fx, self.y, self.c),
            device(self.z, self.x, self.fy, self.c),
            device(self.z, self.x, self.y, self.fc),
        ]
        for partner in partners:
            pl.semaphore_signal(barrier, inc=1, device_id=partner, device_id_type=MESH)
        pl.semaphore_wait(barrier, len(partners))


def device(z, x, y, c):
    return (z * 2 + x, y * 2 + c)


def block_at(z, x, y, c):
    return (z * 2 + x) * 4 + y * 2 + c


def gather_kernel(
    nz,
    own_ref,
    routes_ref,
    x_out,
    mix_ref,
    out_ref,
    stage,
    stage_sem,
    send_sem,
    recv_sem,
    core_sem,
    local_sem,
):
    at = Grid(nz)
    rows, width = own_ref.shape
    half = rows // 2
    experts, slots = stage.shape[1], stage.shape[2]
    at.meet()
    sends = []

    def send(src, dst, sem, to, when):
        copy = pltpu.make_async_remote_copy(
            src_ref=src,
            dst_ref=dst,
            send_sem=send_sem.at[len(sends)],
            recv_sem=sem,
            device_id=to,
            device_id_type=MESH,
        )
        sends.append((when, copy))
        if when is None:
            copy.start()
        else:
            pl.when(when)(copy.start)

    def rows_of(z, x, y, c, h):
        block = out_ref.at[block_at(z, x, y, c)]
        return block if h is None else block.at[pl.ds(h * half, half)]

    def sem_of(sems, z, x, y, h):
        return sems.at[((z * 2 + x) * 2 + y) * 2 + (0 if h is None else h)]

    def forward(z, x, y, h, to, when=None, src=None):
        ref = rows_of(z, x, y, at.c, h)
        send(ref if src is None else src, ref, sem_of(recv_sem, z, x, y, h), to, when)

    def forward_core(z, x, y, h, src=None):
        ref = rows_of(z, x, y, at.c, h)
        to = device(at.z, at.x, at.y, at.fc)
        send(ref if src is None else src, ref, sem_of(core_sem, z, x, y, h), to, None)

    def arrive(sems, z, x, y, c, h):
        ref = rows_of(z, x, y, c, h)
        pltpu.make_async_copy(ref, ref, sem_of(sems, z, x, y, h)).wait()

    local = pltpu.make_async_copy(own_ref, out_ref.at[block_at(at.z, at.x, at.y, at.c)], local_sem)
    local.start()
    to_x = device(at.z, at.fx, at.y, at.c)
    to_y = device(at.z, at.x, at.fy, at.c)
    to_up = device(jnp.minimum(at.z + 1, nz - 1), at.x, at.y, at.c)
    to_down = device(jnp.maximum(at.z - 1, 0), at.x, at.y, at.c)
    more_up, more_down = at.z < nz - 1, at.z > 0

    def spread(z, src=None):
        forward(z, at.x, at.y, None, to_x, None, src)
        forward(z, at.x, at.y, None, to_y, None, src)
        forward_core(z, at.x, at.y, None, src)

    forward(at.z, at.x, at.y, None, to_up, more_up, own_ref)
    forward(at.z, at.x, at.y, None, to_down, more_down, own_ref)
    spread(at.z, own_ref)

    def nearest(k):
        reach = jnp.minimum(at.z, nz - 1 - at.z)
        both = k < 2 * reach
        far = k - reach + 1
        low = jnp.where(both, k % 2 == 0, at.z > reach)
        distance = jnp.where(both, k // 2 + 1, far)
        return jnp.where(low, at.z - distance, at.z + distance), low

    def column(k):
        z, low = nearest(k)
        arrive(recv_sem, z, at.x, at.y, at.c, None)
        forward(z, at.x, at.y, None, to_up, low & more_up)
        forward(z, at.x, at.y, None, to_down, jnp.logical_not(low) & more_down)
        spread(z)

    def turned(z):
        arrive(recv_sem, z, at.fx, at.y, at.c, None)
        forward(z, at.fx, at.y, 0, to_y)
        forward_core(z, at.fx, at.y, None)
        arrive(recv_sem, z, at.x, at.fy, at.c, None)
        forward(z, at.x, at.fy, 1, to_x)
        forward_core(z, at.x, at.fy, None)

    row = lax.broadcasted_iota(jnp.int32, (rows, rows), 0)
    col = lax.broadcasted_iota(jnp.int32, (rows, rows), 1)
    before = (row < col).astype(jnp.bfloat16)
    ctx = lax.axis_index("ctx")
    own = (lax.broadcasted_iota(jnp.int32, (experts, rows), 0) + ctx * experts).astype(jnp.float32)
    spot = lax.broadcasted_iota(jnp.int32, (experts, slots, rows), 1).astype(jnp.float32)
    drains = []

    def dispatch(z, x, y, c):
        b = block_at(z, x, y, c)
        turn = len(drains) % 2
        if len(drains) >= 2:
            drains[-2].wait()
        info = routes_ref[b].astype(jnp.float32)
        hits = jnp.zeros((experts, rows), jnp.float32)
        gates = jnp.zeros((experts, rows), jnp.float32)
        for k in range(TOPK):
            same = info[k : k + 1, :] == own
            hits = jnp.where(same, 1.0, hits)
            gates = jnp.where(same, info[TOPK + k : TOPK + k + 1, :], gates)
        slot = jnp.dot(hits.astype(jnp.bfloat16), before, preferred_element_type=jnp.float32)
        slot = jnp.where(hits > 0, slot, -1.0)
        placed = jnp.where(slot[:, None, :] == spot, 1.0, 0.0)
        weighed = (placed * gates[:, None, :]).reshape(experts * slots, rows)
        mix_ref[b] = weighed.T.astype(jnp.bfloat16)
        placed = placed.reshape(experts * slots, rows).astype(jnp.bfloat16)

        @pl.loop(0, width // 512)
        def _(k):
            cols = pl.ds(pl.multiple_of(k * 512, 512), 512)
            picked = jnp.dot(placed, out_ref[b, :, cols], preferred_element_type=jnp.float32)
            stage[turn, :, :, cols] = picked.astype(stage.dtype).reshape(experts, slots, 512)

        start = pl.multiple_of(b * slots, slots)
        copy = pltpu.make_async_copy(
            stage.at[turn], x_out.at[:, pl.ds(start, slots), :], stage_sem.at[turn]
        )
        copy.start()
        drains.append(copy)

    ready, late = [], []

    def work(count, *blocks):
        late.append(blocks)
        ready.extend((spot, False) for spot in blocks)
        if len(late) > 2:
            ready.extend((spot, True) for spot in late.pop(0))
        for _ in range(min(count, len(ready))):
            (z, x, y, parts), other = ready.pop(0)
            if other:
                for h in parts:
                    arrive(core_sem, z, x, y, at.fc, h)
            dispatch(z, x, y, at.fc if other else at.c)

    local.wait()
    column(0)
    near = [at.z] + [nearest(k)[0] for k in range(nz - 1)]
    work(1, (near[0], at.x, at.y, (None,)))
    turned(at.z)
    work(
        1,
        (near[1], at.x, at.y, (None,)),
        (near[0], at.fx, at.y, (None,)),
        (near[0], at.x, at.fy, (None,)),
    )
    for k in range(1, nz - 1):
        column(k)
        work(2, (near[k + 1], at.x, at.y, (None,)))
    for z in near[1:]:
        turned(z)
        work(2, (z, at.fx, at.y, (None,)), (z, at.x, at.fy, (None,)))
    for z in near:
        for h in range(2):
            arrive(recv_sem, z, at.fx, at.fy, at.c, h)
            forward_core(z, at.fx, at.fy, h)
        work(3, (z, at.fx, at.fy, (0, 1)))
    while late:
        ready.extend((spot, True) for spot in late.pop(0))
    while ready:
        (z, x, y, parts), other = ready.pop(0)
        if other:
            for h in parts:
                arrive(core_sem, z, x, y, at.fc, h)
        dispatch(z, x, y, at.fc if other else at.c)
    for copy in drains[-2:]:
        copy.wait()
    for when, copy in sends:
        if when is None:
            copy.wait_send()
        else:
            pl.when(when)(copy.wait_send)


def gather_rows(own, routes, experts, slots, nz):
    rows, width = own.shape
    blocks = nz * 8
    return pl.pallas_call(
        functools.partial(gather_kernel, nz),
        out_shape=(
            jax.ShapeDtypeStruct((experts, blocks * slots, width), own.dtype),
            jax.ShapeDtypeStruct((blocks, rows, experts * slots), own.dtype),
        ),
        in_specs=[pl.BlockSpec(memory_space=pltpu.VMEM)] * 2,
        out_specs=(
            pl.BlockSpec(memory_space=pl.ANY),
            pl.BlockSpec(memory_space=pltpu.VMEM),
        ),
        scratch_shapes=[
            pltpu.VMEM((blocks, rows, width), own.dtype),
            pltpu.VMEM((2, experts, slots, width), own.dtype),
            pltpu.SemaphoreType.DMA((2,)),
            pltpu.SemaphoreType.DMA((nz * 16,)),
            pltpu.SemaphoreType.DMA((nz * 8,)),
            pltpu.SemaphoreType.DMA((nz * 8,)),
            pltpu.SemaphoreType.DMA,
        ],
        compiler_params=pltpu.CompilerParams(
            collective_id=0, has_side_effects=True, vmem_limit_bytes=40 * 1024 * 1024
        ),
        name="gather_rows",
    )(own, routes)


def combine_kernel(
    nz,
    combiner_ref,
    outs_ref,
    mix_ref,
    acc,
    core_in,
    diag_in,
    x_in,
    y_in,
    z_in,
    stage,
    stage_sem,
    send_sem,
    recv_sem,
    core_sem,
):
    at = Grid(nz)
    rows = acc.shape[1]
    half = rows // 2
    lead = 1
    spots = []
    for z in range(1, nz + 2 * lead + 1):
        spots += [(z, 1, 1)] if z <= nz else []
        spots += [(z - lead, 1, 0), (z - lead, 0, 1)] if 1 <= z - lead <= nz else []
        spots += [(z - 2 * lead, 0, 0)] if z > 2 * lead else []
    sends = []

    def where(spot):
        dz, dx, dy = spot
        return (
            at.turn(dz % nz),
            at.fx if dx else at.x,
            at.fy if dy else at.y,
        )

    def place(z, x, y):
        return (z * 2 + x) * 2 + y

    ahead = 3
    turns = [(spot, at.fc) for spot in spots[:ahead]]
    for i, spot in enumerate(spots):
        turns.append((spot, at.c))
        if i + ahead < len(spots):
            turns.append((spots[i + ahead], at.fc))

    def load(i):
        spot, c = turns[i]
        return pltpu.make_async_copy(
            outs_ref.at[block_at(*where(spot), c)], stage.at[i % 3], stage_sem.at[i % 3]
        )

    load(0).start()
    load(1).start()
    at.meet()

    def send(src, dst, sem, to):
        copy = pltpu.make_async_remote_copy(
            src_ref=src,
            dst_ref=dst,
            send_sem=send_sem.at[len(sends)],
            recv_sem=sem,
            device_id=to,
            device_id_type=MESH,
        )
        copy.start()
        sends.append(copy)

    def arrive(ref, sem):
        pltpu.make_async_copy(ref, ref, sem).wait()

    def make(i):
        if i + 2 < len(turns):
            load(i + 2).start()
        load(i).wait()
        spot, c = turns[i]
        block = block_at(*where(spot), c)
        slot = i % 3

        @pl.loop(0, acc.shape[2] // 512)
        def _(k):
            cols = pl.ds(pl.multiple_of(k * 512, 512), 512)
            acc[block, :, cols] = jnp.dot(
                combiner_ref[block], stage[slot, :, cols], preferred_element_type=jnp.float32
            ).astype(acc.dtype)

        return block

    def add(block, h, others):
        first, count = (0, rows) if h is None else (h * half, half)

        @pl.loop(0, count // 16)
        def _(k):
            at_acc = pl.ds(pl.multiple_of(first + k * 16, 16), 16)
            total = acc[block, at_acc, :].astype(jnp.float32)
            for ref, lead in others:
                total = total + ref[lead, at_acc, :].astype(jnp.float32)
            acc[block, at_acc, :] = total.astype(acc.dtype)

    to_x = device(at.z, at.fx, at.y, at.c)
    to_y = device(at.z, at.x, at.fy, at.c)
    to_core = device(at.z, at.x, at.y, at.fc)
    made = 0

    def give(i):
        spare = place(*where(spots[i]))
        theirs = make(made)
        send(acc.at[theirs], core_in.at[spare], core_sem.at[spare], to_core)

    for i in range(ahead):
        give(i)
        made += 1
    for i, spot in enumerate(spots):
        dz, dx, dy = spot
        z, x, y = where(spot)
        spare = place(z, x, y)
        mine = make(made)
        made += 1
        if i + ahead < len(spots):
            give(i + ahead)
            made += 1
        arrive(core_in.at[spare], core_sem.at[spare])
        if dx and dy:
            add(mine, None, [(core_in, spare)])
            send(
                acc.at[mine, pl.ds(0, half)],
                diag_in.at[z, pl.ds(0, half)],
                recv_sem.at[z],
                to_y,
            )
            send(
                acc.at[mine, pl.ds(half, half)],
                diag_in.at[z, pl.ds(half, half)],
                recv_sem.at[nz + z],
                to_x,
            )
        elif dx:
            arrive(diag_in.at[z, pl.ds(0, half)], recv_sem.at[z])
            add(mine, 0, [(core_in, spare), (diag_in, z)])
            add(mine, 1, [(core_in, spare)])
            send(acc.at[mine], x_in.at[z], recv_sem.at[2 * nz + z], to_x)
        elif dy:
            arrive(diag_in.at[z, pl.ds(half, half)], recv_sem.at[nz + z])
            add(mine, 0, [(core_in, spare)])
            add(mine, 1, [(core_in, spare), (diag_in, z)])
            send(acc.at[mine], y_in.at[z], recv_sem.at[3 * nz + z], to_y)
        else:
            arrive(x_in.at[z], recv_sem.at[2 * nz + z])
            arrive(y_in.at[z], recv_sem.at[3 * nz + z])
            add(mine, None, [(core_in, spare), (x_in, z), (y_in, z)])
            if dz % nz:
                send(
                    acc.at[mine],
                    z_in.at[at.z],
                    recv_sem.at[4 * nz + at.z],
                    device(z, at.x, at.y, at.c),
                )
    others = [at.turn(dz) for dz in range(1, nz)]
    for z in others:
        arrive(z_in.at[z], recv_sem.at[4 * nz + z])
    own = block_at(at.z, at.x, at.y, at.c)

    @pl.loop(0, rows // 16)
    def _(k):
        part = pl.ds(pl.multiple_of(k * 16, 16), 16)
        total = acc[own, part, :].astype(jnp.float32)
        for z in others:
            total = total + z_in[z, part, :].astype(jnp.float32)
        mix_ref[part, :] = total

    for copy in sends:
        copy.wait_send()


def combine_rows(combiner, outs, nz):
    blocks, rows, slots = combiner.shape
    width = outs.shape[2]
    kind = outs.dtype
    return pl.pallas_call(
        functools.partial(combine_kernel, nz),
        out_shape=jax.ShapeDtypeStruct((rows, width), jnp.float32),
        in_specs=[pl.BlockSpec(memory_space=pltpu.VMEM), pl.BlockSpec(memory_space=pl.ANY)],
        out_specs=pl.BlockSpec(memory_space=pltpu.VMEM),
        scratch_shapes=[
            pltpu.VMEM((blocks, rows, width), kind),
            pltpu.VMEM((blocks // 2, rows, width), kind),
            pltpu.VMEM((nz, rows, width), kind),
            pltpu.VMEM((nz, rows, width), kind),
            pltpu.VMEM((nz, rows, width), kind),
            pltpu.VMEM((nz, rows, width), kind),
            pltpu.VMEM((3, slots, width), kind),
            pltpu.SemaphoreType.DMA((3,)),
            pltpu.SemaphoreType.DMA((nz * 10,)),
            pltpu.SemaphoreType.DMA((nz * 5,)),
            pltpu.SemaphoreType.DMA((nz * 4,)),
        ],
        compiler_params=pltpu.CompilerParams(
            collective_id=1, has_side_effects=True, vmem_limit_bytes=56 * 1024 * 1024
        ),
        name="combine_rows",
    )(combiner, outs)


def share_kernel(
    nz, route_ref, state_ref, routes_ref, states_ref, send_sem, z_sem, x_sem, small_sem, far_sem
):
    at = Grid(nz)
    routes_ref[at.z, at.x, at.y, at.c] = route_ref[...]
    states_ref[at.z, at.x] = state_ref[...]
    at.meet()
    sends = []

    def send(ref, sem, to):
        copy = pltpu.make_async_remote_copy(
            src_ref=ref,
            dst_ref=ref,
            send_sem=send_sem.at[len(sends)],
            recv_sem=sem,
            device_id=to,
            device_id_type=MESH,
        )
        copy.start()
        sends.append(copy)

    def arrive(ref, sem):
        pltpu.make_async_copy(ref, ref, sem).wait()

    to_x = device(at.z, at.fx, at.y, at.c)
    to_y = device(at.z, at.x, at.fy, at.c)
    to_core = device(at.z, at.x, at.y, at.fc)
    send(routes_ref.at[at.z, at.x, at.y, at.c], small_sem.at[0], to_x)
    send(states_ref.at[at.z, at.x], x_sem.at[at.z], to_x)
    for dz in range(1, nz):
        send(
            states_ref.at[at.z, at.x], z_sem.at[at.z], device(at.turn(dz), at.x, at.y, at.c)
        )
    arrive(routes_ref.at[at.z, at.fx, at.y, at.c], small_sem.at[0])
    send(routes_ref.at[at.z, :, at.y, at.c], small_sem.at[1], to_y)
    arrive(routes_ref.at[at.z, :, at.fy, at.c], small_sem.at[1])
    send(routes_ref.at[at.z, :, :, at.c], small_sem.at[2], to_core)
    arrive(routes_ref.at[at.z, :, :, at.fc], small_sem.at[2])
    for dz in range(1, nz):
        send(routes_ref.at[at.z], far_sem.at[at.z], device(at.turn(dz), at.x, at.y, at.c))
    for dz in range(1, nz):
        z = at.turn(dz)
        arrive(states_ref.at[z, at.x], z_sem.at[z])
        send(states_ref.at[z, at.x], x_sem.at[z], to_x)
    for dz in range(nz):
        z = at.turn(dz)
        arrive(states_ref.at[z, at.fx], x_sem.at[z])
        if dz:
            arrive(routes_ref.at[z], far_sem.at[z])
    for copy in sends:
        copy.wait_send()


def share(route, state, nz):
    routes, states = pl.pallas_call(
        functools.partial(share_kernel, nz),
        out_shape=(
            jax.ShapeDtypeStruct((nz, 2, 2, 2) + route.shape, route.dtype),
            jax.ShapeDtypeStruct((nz, 2) + state.shape, state.dtype),
        ),
        in_specs=[pl.BlockSpec(memory_space=pltpu.VMEM)] * 2,
        out_specs=(pl.BlockSpec(memory_space=pltpu.VMEM),) * 2,
        scratch_shapes=[
            pltpu.SemaphoreType.DMA((3 * nz + 4,)),
            pltpu.SemaphoreType.DMA((nz,)),
            pltpu.SemaphoreType.DMA((nz,)),
            pltpu.SemaphoreType.DMA((3,)),
            pltpu.SemaphoreType.DMA((nz,)),
        ],
        compiler_params=pltpu.CompilerParams(collective_id=2, has_side_effects=True),
        name="share",
    )(route, state)
    return routes.reshape((nz * 8,) + route.shape), states.reshape((nz * 2,) + state.shape)


def expert_kernel(slots, x_ref, gate_ref, up_ref, down_ref, out_ref):
    total = x_ref.shape[1]
    part = min(total, 512)
    across = (((1,), (1,)), ((), ()))
    for p in range(0, total, part):
        x = x_ref[0, p : p + part, :]
        gate = lax.dot_general(x, gate_ref[0], across, preferred_element_type=jnp.float32)
        up = lax.dot_general(x, up_ref[0], across, preferred_element_type=jnp.float32)
        hidden = (jax.nn.silu(gate) * up).astype(jnp.bfloat16)
        made = jnp.dot(hidden, down_ref[0], preferred_element_type=jnp.float32)
        out_ref[p // slots : (p + part) // slots, 0] = made.astype(jnp.bfloat16).reshape(
            part // slots, slots, made.shape[1]
        )


def run_experts(picked, gate_proj, up_proj, down_proj, slots):
    experts, total, width = picked.shape
    units = gate_proj.shape[2]
    blocks = total // slots
    turn = lambda e: (e, 0, 0)
    out = pl.pallas_call(
        functools.partial(expert_kernel, slots),
        grid=(experts,),
        out_shape=jax.ShapeDtypeStruct((blocks, experts, slots, width), jnp.bfloat16),
        in_specs=[
            pl.BlockSpec((1, total, width), turn),
            pl.BlockSpec((1, units, width), turn),
            pl.BlockSpec((1, units, width), turn),
            pl.BlockSpec((1, units, width), turn),
        ],
        out_specs=pl.BlockSpec((blocks, 1, slots, width), lambda e: (0, e, 0, 0)),
        compiler_params=pltpu.CompilerParams(
            dimension_semantics=("arbitrary",), vmem_limit_bytes=40 * 1024 * 1024
        ),
        name="run_experts",
    )(picked, jnp.swapaxes(gate_proj, 1, 2), jnp.swapaxes(up_proj, 1, 2), down_proj)
    return out.reshape(blocks, experts * slots, width)


def pack_route(expert_ids, gate_weights):
    info = jnp.concatenate([expert_ids.astype(jnp.bfloat16), gate_weights.astype(jnp.bfloat16)], 1)
    return jnp.pad(info.T, ((0, 16 - 2 * TOPK), (0, 0)))


def pack_state(total, state, norm):
    high = total.astype(jnp.bfloat16)
    low = (total - high.astype(jnp.float32)).astype(jnp.bfloat16)
    wide = lambda one: jnp.broadcast_to(one[:, None, None], (one.shape[0], 1, HD))
    packed = jnp.concatenate(
        [state.astype(jnp.bfloat16), norm.astype(jnp.bfloat16)[:, None], wide(high), wide(low)], 1
    )
    return jnp.pad(packed, ((0, 0), (0, 13), (0, 0)))


def prior_of(packs):
    count, index = packs.shape[0], lax.axis_index("ctx")
    totals = packs[:, :, HD + 1, 0].astype(jnp.float32) + packs[:, :, HD + 2, 0].astype(jnp.float32)
    of = jnp.arange(count)
    between = (of[None, :] > of[:, None]) & (of[None, :] < index)
    spans = jnp.sum(jnp.where(between[:, :, None], totals[None], 0.0), axis=1)
    factor = jnp.where((of < index)[:, None], jnp.exp(spans), 0.0)
    prior = jnp.sum(factor[:, :, None, None] * packs[:, :, : HD + 1].astype(jnp.float32), axis=0)
    return prior[:, :HD], prior[:, HD]


def feature_map(values):
    return (jax.nn.elu(values.astype(jnp.float32)) + 1.0).astype(jnp.bfloat16)


def summarize(feat_key, value_rows, log_decay):
    cumulative = jnp.cumsum(log_decay, axis=1)
    block_total = cumulative[:, -1]
    trailing_keys = (
        feat_key.astype(jnp.float32) * jnp.exp(block_total[:, None] - cumulative).T[:, :, None]
    )
    shard_state = jnp.einsum(
        "jfi,jfx->fix",
        trailing_keys.astype(jnp.bfloat16),
        value_rows,
        preferred_element_type=jnp.float32,
    )
    local_norm = jnp.sum(trailing_keys, axis=0)
    return (cumulative, block_total, shard_state, local_norm)


def block_output(feat_query, feat_key, value_rows, cumulative, preceding_state, prior_norm):
    length = feat_query.shape[0]
    scores = jnp.einsum("thd,shd->hts", feat_query, feat_key, preferred_element_type=jnp.float32)
    row_index = lax.broadcasted_iota(jnp.int32, (length, length), 0)
    col_index = lax.broadcasted_iota(jnp.int32, (length, length), 1)
    causal = (col_index <= row_index)[None]
    spread = cumulative[:, :, None] - cumulative[:, None, :]
    weights = jnp.where(causal, scores * jnp.exp(jnp.where(causal, spread, 0.0)), 0.0)
    inner_den = jnp.sum(weights, axis=2).T
    inner_num = jnp.einsum(
        "hts,shd->thd", weights.astype(jnp.bfloat16), value_rows, preferred_element_type=jnp.float32
    )
    query_damping = feat_query.astype(jnp.float32) * jnp.exp(cumulative).T[:, :, None]
    outer_numerator = jnp.einsum(
        "cnm,nmp->cnp", query_damping, preceding_state, precision=lax.Precision.HIGHEST
    )
    outer_den = jnp.einsum("thk,hk->th", query_damping, prior_norm, precision=lax.Precision.HIGHEST)
    mixed_rows = ((inner_num + outer_numerator) / (inner_den + outer_den)[:, :, None]).astype(
        jnp.bfloat16
    )
    return mixed_rows.reshape(length, -1)


def local_routes(expert_ids, gate_weights, row_count, local_experts, capacity):
    blocks = expert_ids.shape[0] // row_count
    own = lax.axis_index("ctx") * local_experts + jnp.arange(local_experts, dtype=jnp.int32)
    named = (expert_ids[:, :, None] == own).astype(jnp.float32)
    gates = jnp.sum(named * gate_weights.astype(jnp.float32)[:, :, None], axis=1)
    hits = jnp.sum(named, axis=1).reshape(blocks, row_count, local_experts)
    row = lax.broadcasted_iota(jnp.int32, (row_count, row_count), 0)
    col = lax.broadcasted_iota(jnp.int32, (row_count, row_count), 1)
    before = (col < row).astype(jnp.bfloat16)
    slot = jnp.einsum(
        "rs,bse->bre", before, hits.astype(jnp.bfloat16), preferred_element_type=jnp.float32
    )
    placed = jnp.where(
        (slot[:, :, :, None] == jnp.arange(capacity, dtype=jnp.float32)) & (hits[:, :, :, None] > 0),
        1.0,
        0.0,
    )
    combiner = placed * gates.reshape(blocks, row_count, local_experts, 1)
    flat = (blocks, row_count, local_experts * capacity)
    return placed.astype(jnp.bfloat16).reshape(flat), combiner.astype(jnp.bfloat16).reshape(flat)


def on_device(
    query_heads,
    key_heads,
    value_heads,
    log_decay,
    residual,
    out_weight,
    norm_gain,
    expert_ids,
    gate_weights,
    gate_proj,
    up_proj,
    down_proj,
):
    length = query_heads.shape[0]
    local_heads = query_heads.shape[1] // HD
    feat_query = feature_map(query_heads).reshape(length, local_heads, HD)
    feat_key = feature_map(key_heads).reshape(length, local_heads, HD)
    value_rows = value_heads.reshape(length, local_heads, HD)
    cumulative, block_total, shard_state, local_norm = summarize(feat_key, value_rows, log_decay)
    row_count = expert_ids.shape[0]
    blocks = lax.axis_size("ctx") * lax.axis_size("grp")
    nz = lax.axis_size("ctx") // 2
    everyone = ("ctx", "grp")
    kernels = lax.axis_size("grp") == 4 and nz > 1 and blocks * row_count <= VMEM_TOKENS
    packed = pack_state(block_total, shard_state, local_norm)
    if kernels:
        routes, packs = share(pack_route(expert_ids, gate_weights), packed, nz)
    else:
        packs = lax.all_gather(packed, "ctx")
    preceding_state, prior_norm = prior_of(packs)
    mixed_rows = block_output(
        feat_query, feat_key, value_rows, cumulative, preceding_state, prior_norm
    )
    head_rows = lax.all_to_all(mixed_rows, "grp", split_axis=0, concat_axis=1, tiled=True)
    projected = jnp.dot(head_rows, out_weight, preferred_element_type=jnp.float32)
    attended = (residual.astype(jnp.float32) + projected).astype(jnp.bfloat16)
    widened = attended.astype(jnp.float32)
    normed = (
        widened * lax.rsqrt(jnp.mean(widened * widened, axis=1, keepdims=True) + 1e-06) * norm_gain
    ).astype(jnp.bfloat16)
    local_experts = gate_proj.shape[0]
    capacity = (5 * row_count * TOPK + 4 * E - 1) // (4 * E)
    capacity = (capacity + 15) // 16 * 16
    if kernels:
        picked, combiner = gather_rows(normed, routes, local_experts, capacity, nz)
        partial_rows = run_experts(picked, gate_proj, up_proj, down_proj, capacity)
        expert_mix = combine_rows(combiner, partial_rows, nz)
    else:
        all_ids = lax.all_gather(expert_ids, everyone, axis=0, tiled=True)
        all_gates = lax.all_gather(gate_weights.astype(jnp.bfloat16), everyone, axis=0, tiled=True)
        placed, combiner = local_routes(all_ids, all_gates, row_count, local_experts, capacity)
        all_rows = lax.all_gather(normed, everyone, axis=0, tiled=True)
        block_rows = jnp.einsum(
            "brs,brd->bsd",
            placed,
            all_rows.reshape(blocks, row_count, D),
            preferred_element_type=jnp.float32,
        ).astype(jnp.bfloat16).reshape(blocks, local_experts, capacity, D)
        gate_part = jnp.einsum(
            "secd,edf->secf", block_rows, gate_proj, preferred_element_type=jnp.float32
        )
        up_part = jnp.einsum(
            "secd,edf->secf", block_rows, up_proj, preferred_element_type=jnp.float32
        )
        hidden = (jax.nn.silu(gate_part) * up_part).astype(jnp.bfloat16)
        partial_out = jnp.einsum(
            "secf,efd->secd", hidden, down_proj, preferred_element_type=jnp.float32
        ).astype(jnp.bfloat16)
        partial_mix = jnp.einsum(
            "brs,bsd->brd",
            combiner,
            partial_out.reshape(blocks, local_experts * capacity, D),
            preferred_element_type=jnp.float32,
        ).astype(jnp.bfloat16)
        expert_mix = lax.psum_scatter(
            partial_mix.reshape(-1, D), everyone, scatter_dimension=0, tiled=True
        ).astype(jnp.float32)
    layer_out = (widened + expert_mix).astype(jnp.bfloat16)
    return (attended, layer_out)


def solution(mesh):
    placed = (
        P("ctx", "grp"),
        P("ctx", "grp"),
        P("ctx", "grp"),
        P("grp", "ctx"),
        P(("ctx", "grp"), None),
        P(),
        P(),
        P(("ctx", "grp"), None),
        P(("ctx", "grp"), None),
        P("ctx", None, "grp"),
        P("ctx", None, "grp"),
        P("ctx", "grp", None),
    )
    return jax.shard_map(
        on_device,
        mesh=mesh,
        in_specs=placed,
        out_specs=(P(("ctx", "grp"), None), P(("ctx", "grp"), None)),
        check_vma=False,
    )
```

```python
import functools

import jax
import jax.numpy as jnp
from jax import lax
from jax.experimental import pallas as pl
from jax.experimental.pallas import tpu as pltpu
from jax.sharding import PartitionSpec as P

D = 2048
HD = 128
E = 64
TOPK = 6


MESH = pl.DeviceIdType.MESH
VMEM_TOKENS = 4096


class Grid:
    def __init__(self, nz):
        ctx, grp = lax.axis_index("ctx"), lax.axis_index("grp")
        self.nz = nz
        self.z, self.x = ctx // 2, ctx % 2
        self.y, self.c = grp // 2, grp % 2
        self.fx, self.fy, self.fc = 1 - self.x, 1 - self.y, 1 - self.c

    def turn(self, dz):
        return lax.rem(self.z + dz, self.nz)

    def meet(self):
        barrier = pltpu.get_barrier_semaphore()
        partners = [device(self.turn(dz), self.x, self.y, self.c) for dz in range(1, self.nz)]
        partners += [
            device(self.z, self.fx, self.y, self.c),
            device(self.z, self.x, self.fy, self.c),
            device(self.z, self.x, self.y, self.fc),
        ]
        for partner in partners:
            pl.semaphore_signal(barrier, inc=1, device_id=partner, device_id_type=MESH)
        pl.semaphore_wait(barrier, len(partners))


def device(z, x, y, c):
    return (z * 2 + x, y * 2 + c)


def block_at(z, x, y, c):
    return (z * 2 + x) * 4 + y * 2 + c


def gather_kernel(
    nz,
    own_ref,
    routes_ref,
    x_out,
    mix_ref,
    out_ref,
    stage,
    stage_sem,
    send_sem,
    recv_sem,
    core_sem,
    local_sem,
):
    at = Grid(nz)
    rows, width = own_ref.shape
    half = rows // 2
    experts, slots = stage.shape[1], stage.shape[2]
    at.meet()
    sends = []

    def send(src, dst, sem, to, when):
        copy = pltpu.make_async_remote_copy(
            src_ref=src,
            dst_ref=dst,
            send_sem=send_sem.at[len(sends)],
            recv_sem=sem,
            device_id=to,
            device_id_type=MESH,
        )
        sends.append((when, copy))
        if when is None:
            copy.start()
        else:
            pl.when(when)(copy.start)

    def rows_of(z, x, y, c, h):
        block = out_ref.at[block_at(z, x, y, c)]
        return block if h is None else block.at[pl.ds(h * half, half)]

    def sem_of(sems, z, x, y, h):
        return sems.at[((z * 2 + x) * 2 + y) * 2 + (0 if h is None else h)]

    def forward(z, x, y, h, to, when=None, src=None):
        ref = rows_of(z, x, y, at.c, h)
        send(ref if src is None else src, ref, sem_of(recv_sem, z, x, y, h), to, when)

    def forward_core(z, x, y, h, src=None):
        ref = rows_of(z, x, y, at.c, h)
        to = device(at.z, at.x, at.y, at.fc)
        send(ref if src is None else src, ref, sem_of(core_sem, z, x, y, h), to, None)

    def arrive(sems, z, x, y, c, h):
        ref = rows_of(z, x, y, c, h)
        pltpu.make_async_copy(ref, ref, sem_of(sems, z, x, y, h)).wait()

    local = pltpu.make_async_copy(own_ref, out_ref.at[block_at(at.z, at.x, at.y, at.c)], local_sem)
    local.start()
    to_x = device(at.z, at.fx, at.y, at.c)
    to_y = device(at.z, at.x, at.fy, at.c)
    to_up = device(jnp.minimum(at.z + 1, nz - 1), at.x, at.y, at.c)
    to_down = device(jnp.maximum(at.z - 1, 0), at.x, at.y, at.c)
    more_up, more_down = at.z < nz - 1, at.z > 0

    def spread(z, src=None):
        forward(z, at.x, at.y, None, to_x, None, src)
        forward(z, at.x, at.y, None, to_y, None, src)
        forward_core(z, at.x, at.y, None, src)

    forward(at.z, at.x, at.y, None, to_up, more_up, own_ref)
    forward(at.z, at.x, at.y, None, to_down, more_down, own_ref)
    spread(at.z, own_ref)

    def nearest(k):
        reach = jnp.minimum(at.z, nz - 1 - at.z)
        both = k < 2 * reach
        far = k - reach + 1
        low = jnp.where(both, k % 2 == 0, at.z > reach)
        distance = jnp.where(both, k // 2 + 1, far)
        return jnp.where(low, at.z - distance, at.z + distance), low

    def column(k):
        z, low = nearest(k)
        arrive(recv_sem, z, at.x, at.y, at.c, None)
        forward(z, at.x, at.y, None, to_up, low & more_up)
        forward(z, at.x, at.y, None, to_down, jnp.logical_not(low) & more_down)
        spread(z)

    def turned(z):
        arrive(recv_sem, z, at.fx, at.y, at.c, None)
        forward(z, at.fx, at.y, 0, to_y)
        forward_core(z, at.fx, at.y, None)
        arrive(recv_sem, z, at.x, at.fy, at.c, None)
        forward(z, at.x, at.fy, 1, to_x)
        forward_core(z, at.x, at.fy, None)

    row = lax.broadcasted_iota(jnp.int32, (rows, rows), 0)
    col = lax.broadcasted_iota(jnp.int32, (rows, rows), 1)
    before = (row < col).astype(jnp.bfloat16)
    ctx = lax.axis_index("ctx")
    own = (lax.broadcasted_iota(jnp.int32, (experts, rows), 0) + ctx * experts).astype(jnp.float32)
    spot = lax.broadcasted_iota(jnp.int32, (experts, slots, rows), 1).astype(jnp.float32)
    drains = []

    def dispatch(z, x, y, c):
        b = block_at(z, x, y, c)
        turn = len(drains) % 2
        if len(drains) >= 2:
            drains[-2].wait()
        info = routes_ref[b].astype(jnp.float32)
        hits = jnp.zeros((experts, rows), jnp.float32)
        gates = jnp.zeros((experts, rows), jnp.float32)
        for k in range(TOPK):
            same = info[k : k + 1, :] == own
            hits = jnp.where(same, 1.0, hits)
            gates = jnp.where(same, info[TOPK + k : TOPK + k + 1, :], gates)
        slot = jnp.dot(hits.astype(jnp.bfloat16), before, preferred_element_type=jnp.float32)
        slot = jnp.where(hits > 0, slot, -1.0)
        placed = jnp.where(slot[:, None, :] == spot, 1.0, 0.0)
        weighed = (placed * gates[:, None, :]).reshape(experts * slots, rows)
        mix_ref[b] = weighed.T.astype(jnp.bfloat16)
        placed = placed.reshape(experts * slots, rows).astype(jnp.bfloat16)

        @pl.loop(0, width // 512)
        def _(k):
            cols = pl.ds(pl.multiple_of(k * 512, 512), 512)
            picked = jnp.dot(placed, out_ref[b, :, cols], preferred_element_type=jnp.float32)
            stage[turn, :, :, cols] = picked.astype(stage.dtype).reshape(experts, slots, 512)

        start = pl.multiple_of(b * slots, slots)
        copy = pltpu.make_async_copy(
            stage.at[turn], x_out.at[:, pl.ds(start, slots), :], stage_sem.at[turn]
        )
        copy.start()
        drains.append(copy)

    ready, late = [], []

    def work(count, *blocks):
        late.append(blocks)
        ready.extend((spot, False) for spot in blocks)
        if len(late) > 2:
            ready.extend((spot, True) for spot in late.pop(0))
        for _ in range(min(count, len(ready))):
            (z, x, y, parts), other = ready.pop(0)
            if other:
                for h in parts:
                    arrive(core_sem, z, x, y, at.fc, h)
            dispatch(z, x, y, at.fc if other else at.c)

    local.wait()
    column(0)
    near = [at.z] + [nearest(k)[0] for k in range(nz - 1)]
    work(1, (near[0], at.x, at.y, (None,)))
    turned(at.z)
    work(
        1,
        (near[1], at.x, at.y, (None,)),
        (near[0], at.fx, at.y, (None,)),
        (near[0], at.x, at.fy, (None,)),
    )
    for k in range(1, nz - 1):
        column(k)
        work(2, (near[k + 1], at.x, at.y, (None,)))
    for z in near[1:]:
        turned(z)
        work(2, (z, at.fx, at.y, (None,)), (z, at.x, at.fy, (None,)))
    for z in near:
        for h in range(2):
            arrive(recv_sem, z, at.fx, at.fy, at.c, h)
            forward_core(z, at.fx, at.fy, h)
        work(3, (z, at.fx, at.fy, (0, 1)))
    while late:
        ready.extend((spot, True) for spot in late.pop(0))
    while ready:
        (z, x, y, parts), other = ready.pop(0)
        if other:
            for h in parts:
                arrive(core_sem, z, x, y, at.fc, h)
        dispatch(z, x, y, at.fc if other else at.c)
    for copy in drains[-2:]:
        copy.wait()
    for when, copy in sends:
        if when is None:
            copy.wait_send()
        else:
            pl.when(when)(copy.wait_send)


def gather_rows(own, routes, experts, slots, nz):
    rows, width = own.shape
    blocks = nz * 8
    return pl.pallas_call(
        functools.partial(gather_kernel, nz),
        out_shape=(
            jax.ShapeDtypeStruct((experts, blocks * slots, width), own.dtype),
            jax.ShapeDtypeStruct((blocks, rows, experts * slots), own.dtype),
        ),
        in_specs=[pl.BlockSpec(memory_space=pltpu.VMEM)] * 2,
        out_specs=(
            pl.BlockSpec(memory_space=pl.ANY),
            pl.BlockSpec(memory_space=pltpu.VMEM),
        ),
        scratch_shapes=[
            pltpu.VMEM((blocks, rows, width), own.dtype),
            pltpu.VMEM((2, experts, slots, width), own.dtype),
            pltpu.SemaphoreType.DMA((2,)),
            pltpu.SemaphoreType.DMA((nz * 16,)),
            pltpu.SemaphoreType.DMA((nz * 8,)),
            pltpu.SemaphoreType.DMA((nz * 8,)),
            pltpu.SemaphoreType.DMA,
        ],
        compiler_params=pltpu.CompilerParams(
            collective_id=0, has_side_effects=True, vmem_limit_bytes=40 * 1024 * 1024
        ),
        name="gather_rows",
    )(own, routes)


def combine_kernel(
    nz,
    combiner_ref,
    outs_ref,
    mix_ref,
    acc,
    core_in,
    diag_in,
    x_in,
    y_in,
    z_in,
    stage,
    stage_sem,
    send_sem,
    recv_sem,
    core_sem,
):
    at = Grid(nz)
    rows = acc.shape[1]
    half = rows // 2
    lead = 1
    spots = []
    for z in range(1, nz + 2 * lead + 1):
        spots += [(z, 1, 1)] if z <= nz else []
        spots += [(z - lead, 1, 0), (z - lead, 0, 1)] if 1 <= z - lead <= nz else []
        spots += [(z - 2 * lead, 0, 0)] if z > 2 * lead else []
    sends = []

    def where(spot):
        dz, dx, dy = spot
        return (
            at.turn(dz % nz),
            at.fx if dx else at.x,
            at.fy if dy else at.y,
        )

    def place(z, x, y):
        return (z * 2 + x) * 2 + y

    ahead = 3
    turns = [(spot, at.fc) for spot in spots[:ahead]]
    for i, spot in enumerate(spots):
        turns.append((spot, at.c))
        if i + ahead < len(spots):
            turns.append((spots[i + ahead], at.fc))

    def load(i):
        spot, c = turns[i]
        return pltpu.make_async_copy(
            outs_ref.at[block_at(*where(spot), c)], stage.at[i % 3], stage_sem.at[i % 3]
        )

    load(0).start()
    load(1).start()
    at.meet()

    def send(src, dst, sem, to):
        copy = pltpu.make_async_remote_copy(
            src_ref=src,
            dst_ref=dst,
            send_sem=send_sem.at[len(sends)],
            recv_sem=sem,
            device_id=to,
            device_id_type=MESH,
        )
        copy.start()
        sends.append(copy)

    def arrive(ref, sem):
        pltpu.make_async_copy(ref, ref, sem).wait()

    def make(i):
        if i + 2 < len(turns):
            load(i + 2).start()
        load(i).wait()
        spot, c = turns[i]
        block = block_at(*where(spot), c)
        slot = i % 3

        @pl.loop(0, acc.shape[2] // 512)
        def _(k):
            cols = pl.ds(pl.multiple_of(k * 512, 512), 512)
            acc[block, :, cols] = jnp.dot(
                combiner_ref[block], stage[slot, :, cols], preferred_element_type=jnp.float32
            ).astype(acc.dtype)

        return block

    def add(block, h, others):
        first, count = (0, rows) if h is None else (h * half, half)

        @pl.loop(0, count // 16)
        def _(k):
            at_acc = pl.ds(pl.multiple_of(first + k * 16, 16), 16)
            total = acc[block, at_acc, :].astype(jnp.float32)
            for ref, lead in others:
                total = total + ref[lead, at_acc, :].astype(jnp.float32)
            acc[block, at_acc, :] = total.astype(acc.dtype)

    to_x = device(at.z, at.fx, at.y, at.c)
    to_y = device(at.z, at.x, at.fy, at.c)
    to_core = device(at.z, at.x, at.y, at.fc)
    made = 0

    def give(i):
        spare = place(*where(spots[i]))
        theirs = make(made)
        send(acc.at[theirs], core_in.at[spare], core_sem.at[spare], to_core)

    for i in range(ahead):
        give(i)
        made += 1
    for i, spot in enumerate(spots):
        dz, dx, dy = spot
        z, x, y = where(spot)
        spare = place(z, x, y)
        mine = make(made)
        made += 1
        if i + ahead < len(spots):
            give(i + ahead)
            made += 1
        arrive(core_in.at[spare], core_sem.at[spare])
        if dx and dy:
            add(mine, None, [(core_in, spare)])
            send(
                acc.at[mine, pl.ds(0, half)],
                diag_in.at[z, pl.ds(0, half)],
                recv_sem.at[z],
                to_y,
            )
            send(
                acc.at[mine, pl.ds(half, half)],
                diag_in.at[z, pl.ds(half, half)],
                recv_sem.at[nz + z],
                to_x,
            )
        elif dx:
            arrive(diag_in.at[z, pl.ds(0, half)], recv_sem.at[z])
            add(mine, 0, [(core_in, spare), (diag_in, z)])
            add(mine, 1, [(core_in, spare)])
            send(acc.at[mine], x_in.at[z], recv_sem.at[2 * nz + z], to_x)
        elif dy:
            arrive(diag_in.at[z, pl.ds(half, half)], recv_sem.at[nz + z])
            add(mine, 0, [(core_in, spare)])
            add(mine, 1, [(core_in, spare), (diag_in, z)])
            send(acc.at[mine], y_in.at[z], recv_sem.at[3 * nz + z], to_y)
        else:
            arrive(x_in.at[z], recv_sem.at[2 * nz + z])
            arrive(y_in.at[z], recv_sem.at[3 * nz + z])
            add(mine, None, [(core_in, spare), (x_in, z), (y_in, z)])
            if dz % nz:
                send(
                    acc.at[mine],
                    z_in.at[at.z],
                    recv_sem.at[4 * nz + at.z],
                    device(z, at.x, at.y, at.c),
                )
    others = [at.turn(dz) for dz in range(1, nz)]
    for z in others:
        arrive(z_in.at[z], recv_sem.at[4 * nz + z])
    own = block_at(at.z, at.x, at.y, at.c)

    @pl.loop(0, rows // 16)
    def _(k):
        part = pl.ds(pl.multiple_of(k * 16, 16), 16)
        total = acc[own, part, :].astype(jnp.float32)
        for z in others:
            total = total + z_in[z, part, :].astype(jnp.float32)
        mix_ref[part, :] = total

    for copy in sends:
        copy.wait_send()


def combine_rows(combiner, outs, nz):
    blocks, rows, slots = combiner.shape
    width = outs.shape[2]
    kind = outs.dtype
    return pl.pallas_call(
        functools.partial(combine_kernel, nz),
        out_shape=jax.ShapeDtypeStruct((rows, width), jnp.float32),
        in_specs=[pl.BlockSpec(memory_space=pltpu.VMEM), pl.BlockSpec(memory_space=pl.ANY)],
        out_specs=pl.BlockSpec(memory_space=pltpu.VMEM),
        scratch_shapes=[
            pltpu.VMEM((blocks, rows, width), kind),
            pltpu.VMEM((blocks // 2, rows, width), kind),
            pltpu.VMEM((nz, rows, width), kind),
            pltpu.VMEM((nz, rows, width), kind),
            pltpu.VMEM((nz, rows, width), kind),
            pltpu.VMEM((nz, rows, width), kind),
            pltpu.VMEM((3, slots, width), kind),
            pltpu.SemaphoreType.DMA((3,)),
            pltpu.SemaphoreType.DMA((nz * 10,)),
            pltpu.SemaphoreType.DMA((nz * 5,)),
            pltpu.SemaphoreType.DMA((nz * 4,)),
        ],
        compiler_params=pltpu.CompilerParams(
            collective_id=1, has_side_effects=True, vmem_limit_bytes=56 * 1024 * 1024
        ),
        name="combine_rows",
    )(combiner, outs)


def swap_kernel(count, mixed_ref, out_ref, send_sem, recv_sem):
    ctx, grp = lax.axis_index("ctx"), lax.axis_index("grp")
    rows, width = out_ref.shape[0], mixed_ref.shape[1]
    barrier = pltpu.get_barrier_semaphore()
    others = [lax.rem(grp + d, count) for d in range(1, count)]
    for other in others:
        pl.semaphore_signal(barrier, inc=1, device_id=(ctx, other), device_id_type=MESH)
    pl.semaphore_wait(barrier, count - 1)

    def rows_for(g):
        return pl.ds(pl.multiple_of(g * rows, rows), rows)

    def heads_of(g):
        return pl.ds(pl.multiple_of(g * width, width), width)

    sends = []
    for d, other in enumerate(others):
        copy = pltpu.make_async_remote_copy(
            src_ref=mixed_ref.at[rows_for(other)],
            dst_ref=out_ref.at[:, heads_of(grp)],
            send_sem=send_sem.at[d],
            recv_sem=recv_sem.at[grp],
            device_id=(ctx, other),
            device_id_type=MESH,
        )
        copy.start()
        sends.append(copy)
    out_ref[:, heads_of(grp)] = mixed_ref[rows_for(grp), :]
    for other in others:
        ref = out_ref.at[:, heads_of(other)]
        pltpu.make_async_copy(ref, ref, recv_sem.at[other]).wait()
    for copy in sends:
        copy.wait_send()


def swap_heads(mixed, count):
    rows, width = mixed.shape
    return pl.pallas_call(
        functools.partial(swap_kernel, count),
        out_shape=jax.ShapeDtypeStruct((rows // count, width * count), mixed.dtype),
        in_specs=[pl.BlockSpec(memory_space=pltpu.VMEM)],
        out_specs=pl.BlockSpec(memory_space=pltpu.VMEM),
        scratch_shapes=[
            pltpu.SemaphoreType.DMA((count - 1,)),
            pltpu.SemaphoreType.DMA((count,)),
        ],
        compiler_params=pltpu.CompilerParams(collective_id=3, has_side_effects=True),
        name="swap_heads",
    )(mixed)


def share_kernel(
    nz, route_ref, state_ref, routes_ref, states_ref, send_sem, z_sem, x_sem, small_sem, far_sem
):
    at = Grid(nz)
    routes_ref[at.z, at.x, at.y, at.c] = route_ref[...]
    states_ref[at.z, at.x] = state_ref[...]
    at.meet()
    sends = []

    def send(ref, sem, to):
        copy = pltpu.make_async_remote_copy(
            src_ref=ref,
            dst_ref=ref,
            send_sem=send_sem.at[len(sends)],
            recv_sem=sem,
            device_id=to,
            device_id_type=MESH,
        )
        copy.start()
        sends.append(copy)

    def arrive(ref, sem):
        pltpu.make_async_copy(ref, ref, sem).wait()

    to_x = device(at.z, at.fx, at.y, at.c)
    to_y = device(at.z, at.x, at.fy, at.c)
    to_core = device(at.z, at.x, at.y, at.fc)
    send(routes_ref.at[at.z, at.x, at.y, at.c], small_sem.at[0], to_x)
    send(states_ref.at[at.z, at.x], x_sem.at[at.z], to_x)
    for dz in range(1, nz):
        send(
            states_ref.at[at.z, at.x], z_sem.at[at.z], device(at.turn(dz), at.x, at.y, at.c)
        )
    arrive(routes_ref.at[at.z, at.fx, at.y, at.c], small_sem.at[0])
    send(routes_ref.at[at.z, :, at.y, at.c], small_sem.at[1], to_y)
    arrive(routes_ref.at[at.z, :, at.fy, at.c], small_sem.at[1])
    send(routes_ref.at[at.z, :, :, at.c], small_sem.at[2], to_core)
    arrive(routes_ref.at[at.z, :, :, at.fc], small_sem.at[2])
    for dz in range(1, nz):
        send(routes_ref.at[at.z], far_sem.at[at.z], device(at.turn(dz), at.x, at.y, at.c))
    for dz in range(1, nz):
        z = at.turn(dz)
        arrive(states_ref.at[z, at.x], z_sem.at[z])
        send(states_ref.at[z, at.x], x_sem.at[z], to_x)
    for dz in range(nz):
        z = at.turn(dz)
        arrive(states_ref.at[z, at.fx], x_sem.at[z])
        if dz:
            arrive(routes_ref.at[z], far_sem.at[z])
    for copy in sends:
        copy.wait_send()


def share(route, state, nz):
    routes, states = pl.pallas_call(
        functools.partial(share_kernel, nz),
        out_shape=(
            jax.ShapeDtypeStruct((nz, 2, 2, 2) + route.shape, route.dtype),
            jax.ShapeDtypeStruct((nz, 2) + state.shape, state.dtype),
        ),
        in_specs=[pl.BlockSpec(memory_space=pltpu.VMEM)] * 2,
        out_specs=(pl.BlockSpec(memory_space=pltpu.VMEM),) * 2,
        scratch_shapes=[
            pltpu.SemaphoreType.DMA((3 * nz + 4,)),
            pltpu.SemaphoreType.DMA((nz,)),
            pltpu.SemaphoreType.DMA((nz,)),
            pltpu.SemaphoreType.DMA((3,)),
            pltpu.SemaphoreType.DMA((nz,)),
        ],
        compiler_params=pltpu.CompilerParams(collective_id=2, has_side_effects=True),
        name="share",
    )(route, state)
    return routes.reshape((nz * 8,) + route.shape), states.reshape((nz * 2,) + state.shape)


def expert_kernel(slots, x_ref, gate_ref, up_ref, down_ref, out_ref):
    total = x_ref.shape[1]
    part = min(total, 512)
    across = (((1,), (1,)), ((), ()))
    for p in range(0, total, part):
        x = x_ref[0, p : p + part, :]
        gate = lax.dot_general(x, gate_ref[0], across, preferred_element_type=jnp.float32)
        up = lax.dot_general(x, up_ref[0], across, preferred_element_type=jnp.float32)
        hidden = (jax.nn.silu(gate) * up).astype(jnp.bfloat16)
        made = jnp.dot(hidden, down_ref[0], preferred_element_type=jnp.float32)
        out_ref[p // slots : (p + part) // slots, 0] = made.astype(jnp.bfloat16).reshape(
            part // slots, slots, made.shape[1]
        )


def run_experts(picked, gate_proj, up_proj, down_proj, slots):
    experts, total, width = picked.shape
    units = gate_proj.shape[2]
    blocks = total // slots
    turn = lambda e: (e, 0, 0)
    out = pl.pallas_call(
        functools.partial(expert_kernel, slots),
        grid=(experts,),
        out_shape=jax.ShapeDtypeStruct((blocks, experts, slots, width), jnp.bfloat16),
        in_specs=[
            pl.BlockSpec((1, total, width), turn),
            pl.BlockSpec((1, units, width), turn),
            pl.BlockSpec((1, units, width), turn),
            pl.BlockSpec((1, units, width), turn),
        ],
        out_specs=pl.BlockSpec((blocks, 1, slots, width), lambda e: (0, e, 0, 0)),
        compiler_params=pltpu.CompilerParams(
            dimension_semantics=("arbitrary",), vmem_limit_bytes=40 * 1024 * 1024
        ),
        name="run_experts",
    )(picked, jnp.swapaxes(gate_proj, 1, 2), jnp.swapaxes(up_proj, 1, 2), down_proj)
    return out.reshape(blocks, experts * slots, width)


def pack_route(expert_ids, gate_weights):
    info = jnp.concatenate([expert_ids.astype(jnp.bfloat16), gate_weights.astype(jnp.bfloat16)], 1)
    return jnp.pad(info.T, ((0, 16 - 2 * TOPK), (0, 0)))


def pack_state(total, state, norm):
    high = total.astype(jnp.bfloat16)
    low = (total - high.astype(jnp.float32)).astype(jnp.bfloat16)
    wide = lambda one: jnp.broadcast_to(one[:, None, None], (one.shape[0], 1, HD))
    packed = jnp.concatenate(
        [state.astype(jnp.bfloat16), norm.astype(jnp.bfloat16)[:, None], wide(high), wide(low)], 1
    )
    return jnp.pad(packed, ((0, 0), (0, 13), (0, 0)))


def prior_of(packs):
    count, index = packs.shape[0], lax.axis_index("ctx")
    totals = packs[:, :, HD + 1, 0].astype(jnp.float32) + packs[:, :, HD + 2, 0].astype(jnp.float32)
    of = jnp.arange(count)
    between = (of[None, :] > of[:, None]) & (of[None, :] < index)
    spans = jnp.sum(jnp.where(between[:, :, None], totals[None], 0.0), axis=1)
    factor = jnp.where((of < index)[:, None], jnp.exp(spans), 0.0)
    prior = jnp.sum(factor[:, :, None, None] * packs[:, :, : HD + 1].astype(jnp.float32), axis=0)
    return prior[:, :HD], prior[:, HD]


def feature_map(values):
    return (jax.nn.elu(values.astype(jnp.float32)) + 1.0).astype(jnp.bfloat16)


def summarize(feat_key, value_rows, log_decay):
    cumulative = jnp.cumsum(log_decay, axis=1)
    block_total = cumulative[:, -1]
    trailing_keys = (
        feat_key.astype(jnp.float32) * jnp.exp(block_total[:, None] - cumulative).T[:, :, None]
    )
    shard_state = jnp.einsum(
        "jfi,jfx->fix",
        trailing_keys.astype(jnp.bfloat16),
        value_rows,
        preferred_element_type=jnp.float32,
    )
    local_norm = jnp.sum(trailing_keys, axis=0)
    return (cumulative, block_total, shard_state, local_norm)


def block_output(feat_query, feat_key, value_rows, cumulative, preceding_state, prior_norm):
    length = feat_query.shape[0]
    scores = jnp.einsum("thd,shd->hts", feat_query, feat_key, preferred_element_type=jnp.float32)
    row_index = lax.broadcasted_iota(jnp.int32, (length, length), 0)
    col_index = lax.broadcasted_iota(jnp.int32, (length, length), 1)
    causal = (col_index <= row_index)[None]
    spread = cumulative[:, :, None] - cumulative[:, None, :]
    weights = jnp.where(causal, scores * jnp.exp(jnp.where(causal, spread, 0.0)), 0.0)
    inner_den = jnp.sum(weights, axis=2).T
    inner_num = jnp.einsum(
        "hts,shd->thd", weights.astype(jnp.bfloat16), value_rows, preferred_element_type=jnp.float32
    )
    query_damping = feat_query.astype(jnp.float32) * jnp.exp(cumulative).T[:, :, None]
    outer_numerator = jnp.einsum(
        "cnm,nmp->cnp", query_damping, preceding_state, precision=lax.Precision.HIGHEST
    )
    outer_den = jnp.einsum("thk,hk->th", query_damping, prior_norm, precision=lax.Precision.HIGHEST)
    mixed_rows = ((inner_num + outer_numerator) / (inner_den + outer_den)[:, :, None]).astype(
        jnp.bfloat16
    )
    return mixed_rows.reshape(length, -1)


def local_routes(expert_ids, gate_weights, row_count, local_experts, capacity):
    blocks = expert_ids.shape[0] // row_count
    own = lax.axis_index("ctx") * local_experts + jnp.arange(local_experts, dtype=jnp.int32)
    named = (expert_ids[:, :, None] == own).astype(jnp.float32)
    gates = jnp.sum(named * gate_weights.astype(jnp.float32)[:, :, None], axis=1)
    hits = jnp.sum(named, axis=1).reshape(blocks, row_count, local_experts)
    row = lax.broadcasted_iota(jnp.int32, (row_count, row_count), 0)
    col = lax.broadcasted_iota(jnp.int32, (row_count, row_count), 1)
    before = (col < row).astype(jnp.bfloat16)
    slot = jnp.einsum(
        "rs,bse->bre", before, hits.astype(jnp.bfloat16), preferred_element_type=jnp.float32
    )
    placed = jnp.where(
        (slot[:, :, :, None] == jnp.arange(capacity, dtype=jnp.float32)) & (hits[:, :, :, None] > 0),
        1.0,
        0.0,
    )
    combiner = placed * gates.reshape(blocks, row_count, local_experts, 1)
    flat = (blocks, row_count, local_experts * capacity)
    return placed.astype(jnp.bfloat16).reshape(flat), combiner.astype(jnp.bfloat16).reshape(flat)


def on_device(
    query_heads,
    key_heads,
    value_heads,
    log_decay,
    residual,
    out_weight,
    norm_gain,
    expert_ids,
    gate_weights,
    gate_proj,
    up_proj,
    down_proj,
):
    length = query_heads.shape[0]
    local_heads = query_heads.shape[1] // HD
    feat_query = feature_map(query_heads).reshape(length, local_heads, HD)
    feat_key = feature_map(key_heads).reshape(length, local_heads, HD)
    value_rows = value_heads.reshape(length, local_heads, HD)
    cumulative, block_total, shard_state, local_norm = summarize(feat_key, value_rows, log_decay)
    row_count = expert_ids.shape[0]
    blocks = lax.axis_size("ctx") * lax.axis_size("grp")
    nz = lax.axis_size("ctx") // 2
    everyone = ("ctx", "grp")
    kernels = lax.axis_size("grp") == 4 and nz > 1 and blocks * row_count <= VMEM_TOKENS
    packed = pack_state(block_total, shard_state, local_norm)
    if kernels:
        routes, packs = share(pack_route(expert_ids, gate_weights), packed, nz)
    else:
        packs = lax.all_gather(packed, "ctx")
    preceding_state, prior_norm = prior_of(packs)
    mixed_rows = block_output(
        feat_query, feat_key, value_rows, cumulative, preceding_state, prior_norm
    )
    if kernels:
        head_rows = swap_heads(mixed_rows, lax.axis_size("grp"))
    else:
        head_rows = lax.all_to_all(mixed_rows, "grp", split_axis=0, concat_axis=1, tiled=True)
    projected = jnp.dot(head_rows, out_weight, preferred_element_type=jnp.float32)
    attended = (residual.astype(jnp.float32) + projected).astype(jnp.bfloat16)
    widened = attended.astype(jnp.float32)
    normed = (
        widened * lax.rsqrt(jnp.mean(widened * widened, axis=1, keepdims=True) + 1e-06) * norm_gain
    ).astype(jnp.bfloat16)
    local_experts = gate_proj.shape[0]
    capacity = (5 * row_count * TOPK + 4 * E - 1) // (4 * E)
    capacity = (capacity + 15) // 16 * 16
    if kernels:
        picked, combiner = gather_rows(normed, routes, local_experts, capacity, nz)
        partial_rows = run_experts(picked, gate_proj, up_proj, down_proj, capacity)
        expert_mix = combine_rows(combiner, partial_rows, nz)
    else:
        all_ids = lax.all_gather(expert_ids, everyone, axis=0, tiled=True)
        all_gates = lax.all_gather(gate_weights.astype(jnp.bfloat16), everyone, axis=0, tiled=True)
        placed, combiner = local_routes(all_ids, all_gates, row_count, local_experts, capacity)
        all_rows = lax.all_gather(normed, everyone, axis=0, tiled=True)
        block_rows = jnp.einsum(
            "brs,brd->bsd",
            placed,
            all_rows.reshape(blocks, row_count, D),
            preferred_element_type=jnp.float32,
        ).astype(jnp.bfloat16).reshape(blocks, local_experts, capacity, D)
        gate_part = jnp.einsum(
            "secd,edf->secf", block_rows, gate_proj, preferred_element_type=jnp.float32
        )
        up_part = jnp.einsum(
            "secd,edf->secf", block_rows, up_proj, preferred_element_type=jnp.float32
        )
        hidden = (jax.nn.silu(gate_part) * up_part).astype(jnp.bfloat16)
        partial_out = jnp.einsum(
            "secf,efd->secd", hidden, down_proj, preferred_element_type=jnp.float32
        ).astype(jnp.bfloat16)
        partial_mix = jnp.einsum(
            "brs,bsd->brd",
            combiner,
            partial_out.reshape(blocks, local_experts * capacity, D),
            preferred_element_type=jnp.float32,
        ).astype(jnp.bfloat16)
        expert_mix = lax.psum_scatter(
            partial_mix.reshape(-1, D), everyone, scatter_dimension=0, tiled=True
        ).astype(jnp.float32)
    layer_out = (widened + expert_mix).astype(jnp.bfloat16)
    return (attended, layer_out)


def solution(mesh):
    placed = (
        P("ctx", "grp"),
        P("ctx", "grp"),
        P("ctx", "grp"),
        P("grp", "ctx"),
        P(("ctx", "grp"), None),
        P(),
        P(),
        P(("ctx", "grp"), None),
        P(("ctx", "grp"), None),
        P("ctx", None, "grp"),
        P("ctx", None, "grp"),
        P("ctx", "grp", None),
    )
    return jax.shard_map(
        on_device,
        mesh=mesh,
        in_specs=placed,
        out_specs=(P(("ctx", "grp"), None), P(("ctx", "grp"), None)),
        check_vma=False,
    )
```
